512 devices in a mesh: dp: 64 (over z, x), col: 8 (over y, core).
Axes of the slice: x: 4, y: 4, z: 16, core: 2. Of those that a mesh axis runs over, the one named last changes fastest.
Arguments:
- jacobian: bfloat16 [131072, 4096], P('dp', 'col'), may hold values from -6 to 6
- residual: float32 [131072], P('dp'), may hold values from -6 to 6
- bucket: int32 [131072], P('dp'), may hold values from 0 to 767
- sign_bit: int32 [131072], P('dp'), may hold values from 0 to 1
Outputs:
- update: float32 [4096], P('col')
- sketched: float32 [768, 4096], P('dp', 'col')
The draws below stay inside these ranges and needn't reach their ends.
All inputs are finite; a program needn't handle non-finite values.
Results may differ from the reference program's by a relative error of at most 0.0003.
Values sent between devices are 32-bit elements; how exact they have to be, the bound alone decides.
A program may use at most 64 MiB of HBM per device.

```python
import math
import jax
import jax.numpy as jnp
from jax import lax

PARAMS = 4096
ROWS_DEV = 2048
SKETCH = 768
ALL_ROWS = 131072


def set_ends(values, stream_key, smallest, high):
    longest = values.shape.index(max(values.shape))
    spots = []
    for shift in (0, 1):
        where = [jax.random.randint(jax.random.fold_in(stream_key, axis), (), 0, length) for axis, length in enumerate(values.shape)]
        where[longest] = (where[longest] + shift) % values.shape[longest]
        spots.append(tuple(where))
    return values.at[spots[0]].set(smallest).at[spots[1]].set(high)


def shard_levels(own_key, shape, cuts, smallest, high):
    def one(axis_at, shards_of):
        heights = jax.random.uniform(jax.random.fold_in(jax.random.fold_in(own_key, 6), axis_at), (shards_of,), jnp.float32, smallest / len(cuts), high / len(cuts))
        return jnp.repeat(jnp.exp(heights), shape[axis_at] // shards_of).reshape((-1,) + (1,) * (len(shape) - axis_at - 1))

    level = one(*cuts[0])
    for cut in cuts[1:]:
        level = level * one(*cut)
    return level


def scatter_about(rng, dims, width, limit, cuts=(), kind=jnp.bfloat16):
    array = width * jax.random.normal(rng, dims, jnp.float32)
    if cuts:
        array = array * shard_levels(rng, dims, cuts, -0.22, 0.18)
    return jnp.clip(array, -limit, limit).astype(kind)


def setup_inputs(seed: int = 0) -> dict:
    arg_keys = jax.random.split(jax.random.key(seed), 5)
    jacobian = scatter_about(arg_keys[0], (ALL_ROWS, PARAMS), 1.0, 6.0, ((0, 64), (1, 8)))
    residual = scatter_about(arg_keys[1], (ALL_ROWS,), 1.0, 6.0, ((0, 64),), jnp.float32)
    bucket = set_ends(jax.random.randint(arg_keys[2], (ALL_ROWS,), 0, SKETCH), jax.random.fold_in(arg_keys[2], 1), 0, SKETCH - 1).astype(jnp.int32)
    sign_bit = set_ends(jax.random.randint(arg_keys[3], (ALL_ROWS,), 0, 2), jax.random.fold_in(arg_keys[3], 1), 0, 1).astype(jnp.int32)
    return dict(jacobian=jacobian, residual=residual, bucket=bucket, sign_bit=sign_bit)


def sketch_all(jacobian, residual, bucket, sign_bit):
    sign_values = (2 * sign_bit - 1).astype(jnp.float32)
    block_rows = ROWS_DEV
    block_count = ALL_ROWS // block_rows
    jac_blocks = jacobian.reshape(block_count, block_rows, PARAMS)
    res_blocks = residual.reshape(block_count, block_rows)
    buck_blocks = bucket.reshape(block_count, block_rows)
    sign_blocks = sign_values.reshape(block_count, block_rows)

    def add_block(carry, pieces):
        jac_piece, res_piece, buck_piece, sign_piece = pieces
        weighted = jac_piece.astype(jnp.float32) * sign_piece[:, None]
        total_jac = carry[0] + jax.ops.segment_sum(weighted, buck_piece, num_segments=SKETCH)
        total_res = carry[1] + jax.ops.segment_sum(res_piece * sign_piece, buck_piece, num_segments=SKETCH)
        return ((total_jac, total_res), None)
    start = (jnp.zeros((SKETCH, PARAMS), jnp.float32), jnp.zeros((SKETCH,), jnp.float32))
    (total_jac, total_res), _ = lax.scan(add_block, start, (jac_blocks, res_blocks, buck_blocks, sign_blocks))
    scaling = math.sqrt(SKETCH / ALL_ROWS)
    return (total_jac * scaling, total_res * scaling)

def reference(jacobian, residual, bucket, sign_bit):
    sketched, rhs = sketch_all(jacobian, residual, bucket, sign_bit)
    kernel = jnp.dot(sketched, sketched.T, precision=lax.Precision.HIGHEST) / PARAMS
    kernel = kernel + 0.5 * jnp.eye(SKETCH, dtype=jnp.float32)
    factor = jnp.linalg.cholesky(kernel)
    middle = lax.linalg.triangular_solve(factor, rhs[:, None], left_side=True, lower=True)
    dual_vec = lax.linalg.triangular_solve(factor, middle, left_side=True, lower=True, transpose_a=True)
    update = jnp.dot(sketched.T, dual_vec[:, 0], precision=lax.Precision.HIGHEST) / math.sqrt(PARAMS)
    return (update, sketched)
```

```python
import functools
import math

import jax
import jax.numpy as jnp
from jax import lax
from jax.experimental import pallas as pl
from jax.experimental.pallas import tpu as pltpu
from jax.sharding import PartitionSpec as P

PARAMS = 4096
SKETCH = 768
DEV_ROWS = 2048
DEV_COLS = 512
LANES = 128
CHUNK = 48
GROUPS = DEV_ROWS // LANES
BLOCKS = SKETCH // LANES
TRI_ROWS = 2816
HALF = TRI_ROWS // 2
X_STRIP = HALF // 4
Y_STRIP = X_STRIP // 4
RHS_ROWS = 8
MESH = pl.DeviceIdType.MESH
HIGHEST = lax.Precision.HIGHEST
STOP_TOL = 3e-6
ACCEPT_TOL = 1e-5
ROUND_STEPS = 4
MAX_ROUNDS = 16


def place():
    dp, col = lax.axis_index("dp"), lax.axis_index("col")
    return dict(x=dp % 4, near=(dp // 4) % 4, far=dp // 16, y=col // 2, core=col % 2)


def peer(me, axis, step):
    at = dict(me)
    size = 2 if axis == "core" else 4
    at[axis] = (me[axis] + step) % size
    return (at["far"] * 16 + at["near"] * 4 + at["x"], at["y"] * 2 + at["core"])


def gather_kernel(
    scaling,
    jac_ref,
    res_ref,
    bucket_ref,
    sign_ref,
    tri_ref,
    rhs_ref,
    cols_ref,
    owned_ref,
    hot,
    acc,
    part,
    x_in,
    near_in,
    far_in,
    lhs,
    rhs_t,
    tri,
    core_in,
    kx_out,
    kx_in,
    ky_out,
    ky_in,
    send_sem,
    recv_sem,
):
    me = place()
    barrier = pltpu.get_barrier_semaphore()
    links = [(axis, step) for axis in ("x", "near", "far", "y") for step in (1, 2, 3)] + [("core", 1)]
    for axis, step in links:
        pl.semaphore_signal(barrier, inc=1, device_id=peer(me, axis, step), device_id_type=MESH)

    used = [0]

    def push(src, dst, axis, step):
        slot = used[0]
        used[0] += 1
        copy = pltpu.make_async_remote_copy(
            src_ref=src,
            dst_ref=dst,
            send_sem=send_sem.at[slot],
            recv_sem=recv_sem.at[slot],
            device_id=peer(me, axis, step),
            device_id_type=MESH,
        )
        copy.start()
        return copy

    sent = []

    def arrive(copies):
        for copy in copies:
            copy.wait_recv()
        sent.extend(copies)

    def fill(block, carry):
        chunk = (block % 4) * 4 + block // 4
        rows = lax.broadcasted_iota(jnp.int32, (CHUNK, LANES), 0) + chunk * CHUNK
        first = pl.multiple_of(block * CHUNK, CHUNK)
        total = jnp.zeros((CHUNK, LANES), jnp.float32)
        for group in range(GROUPS):
            signs = (2 * sign_ref[group : group + 1, :] - 1).astype(jnp.float32)
            signed = jnp.where(bucket_ref[group : group + 1, :] == rows, signs, 0.0)
            total = total + signed * res_ref[group : group + 1, :]
            hot[pl.ds(first, CHUNK), group * LANES : (group + 1) * LANES] = signed.astype(jnp.bfloat16)
        acc[pl.ds(first, CHUNK), :] = total
        return carry

    lax.fori_loop(0, SKETCH // CHUNK, fill, 0)

    def multiply(block, carry):
        first = pl.multiple_of(block * 192, 192)
        terms = jnp.dot(hot[pl.ds(first, 192), :], jac_ref[...], preferred_element_type=jnp.float32)
        for lane in range(4):
            part[lane, pl.ds(first, 192), :] = terms[:, lane * LANES : (lane + 1) * LANES]
        return carry

    lax.fori_loop(0, SKETCH // 192, multiply, 0)
    res_row = lax.dot_general(
        jnp.ones((RHS_ROWS, LANES), jnp.float32),
        acc[...],
        (((1,), (1,)), ((), ())),
        precision=HIGHEST,
        preferred_element_type=jnp.float32,
    )
    res_tile = jnp.concatenate(
        [res_row[0:1, i * LANES : (i + 1) * LANES] for i in range(BLOCKS)]
        + [jnp.zeros((RHS_ROWS - BLOCKS, LANES), jnp.float32)],
        axis=0,
    )
    for lane in range(4):
        part[lane, SKETCH:, :] = res_tile

    pl.semaphore_wait(barrier, len(links))

    x = me["x"]
    copies = [push(part.at[(x + s) % 4], x_in.at[x], "x", s) for s in (1, 2, 3)]
    x_in[x] = part[x]
    arrive(copies)
    summed = x_in[0] + x_in[1] + x_in[2] + x_in[3]
    x_sum = part.at[x]
    x_sum[...] = summed

    near = me["near"]
    copies = []
    for s in (1, 2, 3):
        rows = pl.multiple_of((near + s) % 4 * 192, 192)
        copies.append(push(x_sum.at[pl.ds(rows, 192), :], near_in.at[near, 0:192, :], "near", s))
        copies.append(push(x_sum.at[SKETCH:, :], near_in.at[near, 192:, :], "near", s))
    near_in[near, 0:192, :] = part[x, pl.ds(pl.multiple_of(near * 192, 192), 192), :]
    near_in[near, 192:, :] = part[x, SKETCH:, :]
    arrive(copies)
    near_sum = near_in.at[near]
    near_sum[...] = near_in[0] + near_in[1] + near_in[2] + near_in[3]

    far = me["far"]
    copies = []
    for s in (1, 2, 3):
        rows = pl.multiple_of((far + s) % 4 * CHUNK, CHUNK)
        copies.append(push(near_sum.at[pl.ds(rows, CHUNK), :], far_in.at[far, 0:CHUNK, :], "far", s))
        copies.append(push(near_sum.at[192:, :], far_in.at[far, CHUNK:, :], "far", s))
    far_in[far, 0:CHUNK, :] = near_in[near, pl.ds(pl.multiple_of(far * CHUNK, CHUNK), CHUNK), :]
    far_in[far, CHUNK:, :] = near_in[near, 192:, :]
    arrive(copies)
    total = (far_in[0] + far_in[1] + far_in[2] + far_in[3]) * scaling
    rhs_ref[...] = total[CHUNK:, :]
    mine = pl.multiple_of(near * 192 + far * CHUNK, CHUNK)
    cols_ref[pl.ds(mine, CHUNK), :] = total[0:CHUNK, :]
    owned_ref[x] = total[0:CHUNK, :]

    own = cols_ref.at[pl.ds(mine, CHUNK), :]
    copies = [push(own, own, "far", s) for s in (1, 2, 3)]
    owned_copies = [push(owned_ref.at[x], owned_ref.at[x], "x", s) for s in (1, 2, 3)]
    arrive(copies)
    quarter = cols_ref.at[pl.ds(pl.multiple_of(near * 192, 192), 192), :]
    copies = [push(quarter, quarter, "near", s) for s in (1, 2, 3)]
    arrive(copies)

    values = cols_ref[...]
    high = values.astype(jnp.bfloat16)
    low = (values - high.astype(jnp.float32)).astype(jnp.bfloat16)
    lhs[:, 0:LANES] = high
    lhs[:, LANES : 2 * LANES] = high
    lhs[:, 2 * LANES :] = low
    rhs_t[:, 0:LANES] = high
    rhs_t[:, LANES : 2 * LANES] = low
    rhs_t[:, 2 * LANES :] = high
    base = 0
    for i in range(BLOCKS):
        width = (i + 1) * LANES
        product = lax.dot_general(
            lhs[i * LANES : width, :],
            rhs_t[0:width, :],
            (((1,), (1,)), ((), ())),
            preferred_element_type=jnp.float32,
        )
        for j in range(i + 1):
            tri[base : base + LANES, :] = product[:, j * LANES : (j + 1) * LANES]
            base += LANES
    tri[base:, :] = jnp.zeros((TRI_ROWS - base, LANES), jnp.float32)

    core = me["core"]
    half = pl.multiple_of(core * HALF, HALF)
    other = pl.multiple_of((1 - core) * HALF, HALF)
    arrive([push(tri.at[pl.ds(other, HALF), :], core_in, "core", 1)])
    kx_out[...] = tri[pl.ds(half, HALF), :] + core_in[...]
    copies = []
    for s in (1, 2, 3):
        rows = pl.multiple_of((x + s) % 4 * X_STRIP, X_STRIP)
        copies.append(push(kx_out.at[pl.ds(rows, X_STRIP), :], kx_in.at[x], "x", s))
    kx_in[x] = kx_out[pl.ds(pl.multiple_of(x * X_STRIP, X_STRIP), X_STRIP), :]
    arrive(copies)
    ky_out[...] = kx_in[0] + kx_in[1] + kx_in[2] + kx_in[3]
    y = me["y"]
    copies = []
    for s in (1, 2, 3):
        rows = pl.multiple_of((y + s) % 4 * Y_STRIP, Y_STRIP)
        copies.append(push(ky_out.at[pl.ds(rows, Y_STRIP), :], ky_in.at[y], "y", s))
    ky_in[y] = ky_out[pl.ds(pl.multiple_of(y * Y_STRIP, Y_STRIP), Y_STRIP), :]
    arrive(copies)
    strip = pl.multiple_of(core * HALF + x * X_STRIP + y * Y_STRIP, Y_STRIP)
    tri_ref[pl.ds(strip, Y_STRIP), :] = ky_in[0] + ky_in[1] + ky_in[2] + ky_in[3]

    piece = tri_ref.at[pl.ds(strip, Y_STRIP), :]
    arrive([push(piece, piece, "y", s) for s in (1, 2, 3)])
    piece = tri_ref.at[pl.ds(pl.multiple_of(core * HALF + x * X_STRIP, X_STRIP), X_STRIP), :]
    arrive([push(piece, piece, "x", s) for s in (1, 2, 3)])
    piece = tri_ref.at[pl.ds(half, HALF), :]
    arrive([push(piece, piece, "core", 1)])
    arrive(owned_copies)
    for copy in sent:
        copy.wait_send()


COPIES = 3 + 6 + 6 + 3 + 3 + 3 + 1 + 3 + 3 + 3 + 3 + 1


def gather(jacobian, residual, bucket, sign_bit, scaling):
    f32 = jnp.float32
    return pl.pallas_call(
        functools.partial(gather_kernel, scaling),
        out_shape=(
            jax.ShapeDtypeStruct((TRI_ROWS, LANES), f32),
            jax.ShapeDtypeStruct((RHS_ROWS, LANES), f32),
            jax.ShapeDtypeStruct((SKETCH, LANES), f32),
            jax.ShapeDtypeStruct((4, CHUNK, LANES), f32),
        ),
        in_specs=[pl.BlockSpec(memory_space=pltpu.VMEM)] * 4,
        out_specs=[pl.BlockSpec(memory_space=pltpu.VMEM)] * 4,
        scratch_shapes=[
            pltpu.VMEM((SKETCH, DEV_ROWS), jnp.bfloat16),
            pltpu.VMEM((SKETCH, LANES), f32),
            pltpu.VMEM((4, SKETCH + RHS_ROWS, LANES), f32),
            pltpu.VMEM((4, SKETCH + RHS_ROWS, LANES), f32),
            pltpu.VMEM((4, 192 + RHS_ROWS, LANES), f32),
            pltpu.VMEM((4, CHUNK + RHS_ROWS, LANES), f32),
            pltpu.VMEM((SKETCH, 3 * LANES), jnp.bfloat16),
            pltpu.VMEM((SKETCH, 3 * LANES), jnp.bfloat16),
            pltpu.VMEM((TRI_ROWS, LANES), f32),
            pltpu.VMEM((HALF, LANES), f32),
            pltpu.VMEM((HALF, LANES), f32),
            pltpu.VMEM((4, X_STRIP, LANES), f32),
            pltpu.VMEM((X_STRIP, LANES), f32),
            pltpu.VMEM((4, Y_STRIP, LANES), f32),
            pltpu.SemaphoreType.DMA((COPIES,)),
            pltpu.SemaphoreType.DMA((COPIES,)),
        ],
        compiler_params=pltpu.CompilerParams(
            collective_id=0, has_side_effects=True, vmem_limit_bytes=48 * 1024 * 1024
        ),
        name="sketch_and_kernel",
    )(jacobian, residual, bucket, sign_bit)


def total_of(row):
    return jnp.sum(row, axis=(0, 1), keepdims=True)


def solve_kernel(tri_ref, rhs_ref, cols_ref, out_ref, mat, column, answer):
    base = 0
    eye = (
        lax.broadcasted_iota(jnp.int32, (LANES, LANES), 0) == lax.broadcasted_iota(jnp.int32, (LANES, LANES), 1)
    ).astype(jnp.float32) * 0.5
    for i in range(BLOCKS):
        for j in range(i + 1):
            block = tri_ref[base : base + LANES, :] * (1.0 / PARAMS)
            base += LANES
            if i == j:
                block = block + eye
            mat[i * LANES : (i + 1) * LANES, j * LANES : (j + 1) * LANES] = block
            if i != j:
                mat[j * LANES : (j + 1) * LANES, i * LANES : (i + 1) * LANES] = block.T

    raw = jnp.concatenate([rhs_ref[i : i + 1, :] for i in range(BLOCKS)], axis=1)
    largest = jnp.max(jnp.abs(raw), axis=(0, 1), keepdims=True)
    unit = jnp.where(largest > 0, largest, 1.0)
    rhs = raw / unit

    def to_column(row):
        for i in range(BLOCKS):
            piece = jnp.broadcast_to(row[:, i * LANES : (i + 1) * LANES], (LANES, LANES))
            column[i * LANES : (i + 1) * LANES, :] = piece.T

    def product(row):
        to_column(row)
        sums = [jnp.zeros((8, LANES), jnp.float32) for _ in range(BLOCKS)]
        for group in range(SKETCH // 8):
            rows = slice(group * 8, group * 8 + 8)
            weight = column[rows, :]
            for i in range(BLOCKS):
                sums[i] = sums[i] + weight * mat[rows, i * LANES : (i + 1) * LANES]
        return jnp.concatenate([jnp.sum(s, axis=0, keepdims=True) for s in sums], axis=1)

    def met(sol, res, tol):
        scale = total_of(sol * (rhs - res)) - 0.5 * total_of(sol * sol)
        return (tol * tol * scale - 2.0 * total_of(res * res))[0, 0] >= 0.0

    def step(_, carry):
        sol, res, way, size = carry
        image = product(way)
        curve = total_of(way * image)
        alpha = jnp.where(curve > 0, size / curve, 0.0)
        sol = sol + alpha * way
        res = res - alpha * image
        new_size = total_of(res * res)
        beta = jnp.where(size > 0, new_size / size, 0.0)
        return (sol, res, res + beta * way, new_size)

    def round_of(carry):
        count, _, state = carry
        state = lax.fori_loop(0, ROUND_STEPS, step, state)
        return (count + 1, met(state[0], state[1], STOP_TOL), state)

    def go_on(carry):
        count, done, _ = carry
        return jnp.logical_and(count < MAX_ROUNDS, jnp.logical_not(done))

    start = (jnp.zeros_like(rhs), rhs, rhs, total_of(rhs * rhs))
    first_done = largest[0, 0] <= 0.0
    _, _, (sol, _, _, _) = lax.while_loop(go_on, round_of, (0, first_done, start))
    true_res = rhs - product(sol)
    good = met(sol, true_res, ACCEPT_TOL)
    to_column(sol)
    answer[...] = column[...]

    @pl.when(jnp.logical_not(good))
    def _():
        to_column(rhs)
        answer[...] = column[...]
        lanes = lax.broadcasted_iota(jnp.int32, (8, SKETCH), 1)
        below = lax.broadcasted_iota(jnp.int32, (8, LANES), 0)

        def pivot(k, carry):
            pivot_row = mat[pl.ds(k, 1), :]
            pivot_rhs = answer[pl.ds(k, 1), :]
            inverse = 1.0 / jnp.sum(jnp.where(lanes[0:1] == k, pivot_row, 0.0), axis=1, keepdims=True)

            def rows_of(group, inner):
                first = pl.multiple_of(group * 8, 8)
                here = mat[pl.ds(first, 8), :]
                factor = jnp.sum(jnp.where(lanes == k, here, 0.0), axis=1, keepdims=True) * inverse
                factor = jnp.where(below[:, 0:1] + first == k, 0.0, factor)
                mat[pl.ds(first, 8), :] = here - factor * pivot_row
                answer[pl.ds(first, 8), :] = answer[pl.ds(first, 8), :] - factor * pivot_rhs
                return inner

            return lax.fori_loop(0, SKETCH // 8, rows_of, carry)

        lax.fori_loop(0, SKETCH, pivot, 0)

        def divide(group, carry):
            first = pl.multiple_of(group * 8, 8)
            here = mat[pl.ds(first, 8), :]
            row = lax.broadcasted_iota(jnp.int32, (8, SKETCH), 0) + first
            diagonal = jnp.sum(jnp.where(lanes == row, here, 0.0), axis=1, keepdims=True)
            answer[pl.ds(first, 8), :] = answer[pl.ds(first, 8), :] / diagonal
            return carry

        lax.fori_loop(0, SKETCH // 8, divide, 0)

    values = jnp.sum(answer[...] * cols_ref[...], axis=0, keepdims=True)
    out_ref[...] = jnp.broadcast_to(values * (unit * (1.0 / math.sqrt(PARAMS))), (8, LANES))


def solve(tri, rhs, cols):
    return pl.pallas_call(
        solve_kernel,
        out_shape=jax.ShapeDtypeStruct((8, LANES), jnp.float32),
        in_specs=[pl.BlockSpec(memory_space=pltpu.VMEM)] * 3,
        out_specs=pl.BlockSpec(memory_space=pltpu.VMEM),
        scratch_shapes=[
            pltpu.VMEM((SKETCH, SKETCH), jnp.float32),
            pltpu.VMEM((SKETCH, LANES), jnp.float32),
            pltpu.VMEM((SKETCH, LANES), jnp.float32),
        ],
        compiler_params=pltpu.CompilerParams(vmem_limit_bytes=48 * 1024 * 1024),
        name="solve",
    )(tri, rhs, cols)


def join_kernel(part_ref, out_ref, send_sem, recv_sem):
    me = place()
    barrier = pltpu.get_barrier_semaphore()
    for step in (1, 2, 3):
        pl.semaphore_signal(barrier, inc=1, device_id=peer(me, "x", step), device_id_type=MESH)
    x = me["x"]
    out_ref[x] = part_ref[...]
    pl.semaphore_wait(barrier, 3)
    copies = []
    for step in (1, 2, 3):
        copy = pltpu.make_async_remote_copy(
            src_ref=part_ref,
            dst_ref=out_ref.at[x],
            send_sem=send_sem.at[step - 1],
            recv_sem=recv_sem.at[step - 1],
            device_id=peer(me, "x", step),
            device_id_type=MESH,
        )
        copy.start()
        copies.append(copy)
    for copy in copies:
        copy.wait()


def join(part):
    return pl.pallas_call(
        join_kernel,
        out_shape=jax.ShapeDtypeStruct((4, 8, LANES), jnp.float32),
        in_specs=[pl.BlockSpec(memory_space=pltpu.VMEM)],
        out_specs=pl.BlockSpec(memory_space=pltpu.VMEM),
        scratch_shapes=[pltpu.SemaphoreType.DMA((3,)), pltpu.SemaphoreType.DMA((3,))],
        compiler_params=pltpu.CompilerParams(collective_id=1, has_side_effects=True),
        name="join_update",
    )(part)


def on_device(jacobian, residual, bucket, sign_bit):
    scaling = math.sqrt(SKETCH / (DEV_ROWS * 64))
    tile = (GROUPS, LANES)
    tri, rhs, cols, owned = gather(
        jacobian, residual.reshape(tile), bucket.reshape(tile), sign_bit.reshape(tile), scaling
    )
    update = join(solve(tri, rhs, cols))[:, 0, :].reshape(DEV_COLS)
    chunk = owned.transpose(1, 0, 2).reshape(CHUNK, DEV_COLS)
    rows = lax.dynamic_slice_in_dim(chunk, lax.axis_index("dp") % 4 * 12, 12, 0)
    return (update, rows)


def solution(mesh):
    return jax.shard_map(
        on_device,
        mesh=mesh,
        in_specs=(P("dp", "col"), P("dp"), P("dp"), P("dp")),
        out_specs=(P("col"), P("dp", "col")),
        check_vma=False,
    )
```

```python
import functools
import math

import jax
import jax.numpy as jnp
from jax import lax
from jax.experimental import pallas as pl
from jax.experimental.pallas import tpu as pltpu
from jax.sharding import PartitionSpec as P

PARAMS = 4096
SKETCH = 768
DEV_ROWS = 2048
DEV_COLS = 512
OWN_ROWS = 12
LANES = 128
CHUNK = 48
BLOCK = 4 * CHUNK
GROUPS = DEV_ROWS // LANES
BLOCKS = SKETCH // LANES
TRI_ROWS = 2816
HALF = TRI_ROWS // 2
PART_A = 640
PART_B = HALF - PART_A
RHS_ROWS = 8
MESH = pl.DeviceIdType.MESH
HIGHEST = lax.Precision.HIGHEST
STOP_TOL = 3e-6
ACCEPT_TOL = 1e-5
ROUND_STEPS = 4
MAX_ROUNDS = 16


def place():
    dp, col = lax.axis_index("dp"), lax.axis_index("col")
    return dict(x=dp % 4, near=(dp // 4) % 4, far=dp // 16, y=col // 2, core=col % 2)


def peer(me, axis, step):
    at = dict(me)
    size = 2 if axis == "core" else 4
    at[axis] = (me[axis] + step) % size
    return (at["far"] * 16 + at["near"] * 4 + at["x"], at["y"] * 2 + at["core"])


def gather_kernel(
    scaling,
    jac_hbm,
    res_hbm,
    bucket_hbm,
    sign_hbm,
    tri_ref,
    rhs_ref,
    cols_ref,
    jac_ref,
    res_ref,
    bucket_ref,
    sign_ref,
    hot,
    acc,
    part,
    x_in,
    x_sum,
    near_in,
    near_sum,
    far_in,
    res_x,
    res_near,
    res_far,
    lhs,
    rhs_t,
    tri,
    core_in,
    k_out,
    k_in_a,
    k_in_b,
    l_out_a,
    l_out_b,
    l_in_a,
    l_in_b,
    load_sem,
    send_sem,
    recv_sem,
):
    me = place()
    x, near, far, y, core = (me[name] for name in ("x", "near", "far", "y", "core"))
    barrier = pltpu.get_barrier_semaphore()
    links = [(axis, step) for axis in ("x", "near", "far", "y") for step in (1, 2, 3)] + [("core", 1)]
    for axis, step in links:
        pl.semaphore_signal(barrier, inc=1, device_id=peer(me, axis, step), device_id_type=MESH)

    loads = [
        pltpu.make_async_copy(src, dst, load_sem.at[i])
        for i, (src, dst) in enumerate(
            [(bucket_hbm, bucket_ref), (sign_hbm, sign_ref), (res_hbm, res_ref), (jac_hbm, jac_ref)]
        )
    ]
    for load in loads:
        load.start()

    used = [0]
    sent = []

    def push(src, dst, axis, step):
        slot = used[0]
        used[0] += 1
        copy = pltpu.make_async_remote_copy(
            src_ref=src,
            dst_ref=dst,
            send_sem=send_sem.at[slot],
            recv_sem=recv_sem.at[slot],
            device_id=peer(me, axis, step),
            device_id_type=MESH,
        )
        copy.start()
        sent.append(copy)
        return copy

    def arrive(copies):
        for copy in copies:
            copy.wait_recv()

    def rows_at(first, count, unit=8):
        return pl.ds(pl.multiple_of(first, unit), count)

    def block_at(index):
        return rows_at(index % 4 * BLOCK, BLOCK, BLOCK)

    for load in loads[:3]:
        load.wait()

    def fill(block, carry):
        chunk = (block % 4) * 4 + block // 4
        rows = lax.broadcasted_iota(jnp.int32, (CHUNK, LANES), 0) + chunk * CHUNK
        first = pl.multiple_of(block * CHUNK, CHUNK)
        total = jnp.zeros((CHUNK, LANES), jnp.float32)
        for group in range(GROUPS):
            signs = (2 * sign_ref[group : group + 1, :] - 1).astype(jnp.float32)
            signed = jnp.where(bucket_ref[group : group + 1, :] == rows, signs, 0.0)
            total = total + signed * res_ref[group : group + 1, :]
            hot[pl.ds(first, CHUNK), group * LANES : (group + 1) * LANES] = signed.astype(jnp.bfloat16)
        acc[pl.ds(first, CHUNK), :] = total
        return carry

    lax.fori_loop(0, SKETCH // CHUNK, fill, 0)
    loads[3].wait()

    def multiply(block, carry):
        first = pl.multiple_of(block * BLOCK, BLOCK)
        terms = jnp.dot(hot[pl.ds(first, BLOCK), :], jac_ref[...], preferred_element_type=jnp.float32)
        for lane in range(4):
            part[lane, pl.ds(first, BLOCK), :] = terms[:, lane * LANES : (lane + 1) * LANES]
        return carry

    lax.fori_loop(0, SKETCH // BLOCK, multiply, 0)
    pl.semaphore_wait(barrier, len(links))

    x_copies = []
    for q in range(4):
        rows = block_at(near + 1 + q)
        x_copies.append([push(part.at[(x + s) % 4, rows, :], x_in.at[x, rows, :], "x", s) for s in (2, 1, 3)])

    res_row = lax.dot_general(
        jnp.ones((RHS_ROWS, LANES), jnp.float32),
        acc[...],
        (((1,), (1,)), ((), ())),
        precision=HIGHEST,
        preferred_element_type=jnp.float32,
    )
    res_x[x] = jnp.concatenate(
        [res_row[0:1, i * LANES : (i + 1) * LANES] for i in range(BLOCKS)]
        + [jnp.zeros((RHS_ROWS - BLOCKS, LANES), jnp.float32)],
        axis=0,
    )
    res_copies = [push(res_x.at[x], res_x.at[x], "x", s) for s in (1, 2, 3)]

    near_copies = []
    for q in range(4):
        rows = block_at(near + 1 + q)
        arrive(x_copies[q])
        summed = part[x, rows, :]
        for s in (1, 2, 3):
            summed = summed + x_in[(x + s) % 4, rows, :]
        if q < 3:
            x_sum[rows, :] = summed
            near_copies.append(push(x_sum.at[rows, :], near_in.at[near], "near", q + 1))
        else:
            near_in[near] = summed
        if q == 1:
            arrive(res_copies)
            res_near[near] = res_x[0] + res_x[1] + res_x[2] + res_x[3]
            res_copies = [push(res_near.at[near], res_near.at[near], "near", s) for s in (1, 2, 3)]
    arrive(near_copies)
    near_sum[...] = near_in[0] + near_in[1] + near_in[2] + near_in[3]

    far_copies = []
    for s in (2, 1, 3):
        rows = rows_at((far + s) % 4 * CHUNK, CHUNK, CHUNK)
        far_copies.append(push(near_sum.at[rows, :], far_in.at[far], "far", s))
    far_in[far] = near_sum[rows_at(far * CHUNK, CHUNK, CHUNK), :]
    arrive(res_copies)
    res_far[far] = res_near[0] + res_near[1] + res_near[2] + res_near[3]
    res_copies = [push(res_far.at[far], res_far.at[far], "far", s) for s in (1, 2, 3)]
    arrive(far_copies)

    def chunk_of(at_near, at_far):
        rows = rows_at(at_near % 4 * BLOCK + at_far % 4 * CHUNK, CHUNK, CHUNK)
        return cols_ref.at[x, rows, :]

    own = chunk_of(near, far)
    own[...] = (far_in[0] + far_in[1] + far_in[2] + far_in[3]) * scaling

    far_copies = {s: push(own, own, "far", s) for s in (2, 1, 3)}
    near_copies = [push(own, own, "near", s) for s in (2, 1, 3)]
    cols_copies = [push(own, own, "x", s) for s in (2, 1, 3)]
    arrive(res_copies)
    rhs_ref[...] = (res_far[0] + res_far[1] + res_far[2] + res_far[3]) * scaling
    for s in (1, 3, 2):
        arrive([far_copies[s]])
        chunk = chunk_of(near, far - s + 4)
        near_copies += [push(chunk, chunk, "near", t) for t in (2, 1, 3)]
        cols_copies += [push(chunk, chunk, "x", t) for t in (2, 1, 3)]
    arrive(near_copies)

    def share(step):
        block = cols_ref.at[x, block_at(near + step), :]
        cols_copies.extend([push(block, block, "x", t) for t in (2, 1, 3)])

    share(1)

    values = cols_ref[x]
    high = values.astype(jnp.bfloat16)
    low = (values - high.astype(jnp.float32)).astype(jnp.bfloat16)
    lhs[:, 0:LANES] = high
    lhs[:, LANES : 2 * LANES] = high
    lhs[:, 2 * LANES :] = low
    rhs_t[:, 0:LANES] = high
    rhs_t[:, LANES : 2 * LANES] = low
    rhs_t[:, 2 * LANES :] = high
    base = 0
    for i in range(BLOCKS):
        width = (i + 1) * LANES
        product = lax.dot_general(
            lhs[i * LANES : width, :],
            rhs_t[0:width, :],
            (((1,), (1,)), ((), ())),
            preferred_element_type=jnp.float32,
        )
        for j in range(i + 1):
            tri[base : base + LANES, :] = product[:, j * LANES : (j + 1) * LANES]
            base += LANES
    tri[base:, :] = jnp.zeros((TRI_ROWS - base, LANES), jnp.float32)

    half = core * HALF
    other = (1 - core) * HALF
    spans = ((0, PART_A), (PART_A, PART_B))
    core_copies = [
        push(tri.at[rows_at(other + first, count), :], core_in.at[first : first + count, :], "core", 1)
        for first, count in spans
    ]
    orders = (("x", "y", x, y, k_in_a, l_out_a, l_in_a), ("y", "x", y, x, k_in_b, l_out_b, l_in_b))

    first_copies = []
    for (first, count), copy, (axis, _, index, _, k_in, _, _) in zip(spans, core_copies, orders):
        arrive([copy])
        k_out[first : first + count, :] = tri[rows_at(half + first, count), :] + core_in[first : first + count, :]
        strip = count // 4
        first_copies.append(
            [
                push(k_out.at[rows_at(first + (index + s) % 4 * strip, strip), :], k_in.at[index], axis, s)
                for s in (2, 1, 3)
            ]
        )
        k_in[index] = k_out[rows_at(first + index * strip, strip), :]
    second_copies = []
    for (first, count), copies, (_, axis, _, index, k_in, l_out, l_in) in zip(spans, first_copies, orders):
        strip = count // 16
        arrive(copies)
        l_out[...] = k_in[0] + k_in[1] + k_in[2] + k_in[3]
        second_copies.append(
            [push(l_out.at[rows_at((index + s) % 4 * strip, strip), :], l_in.at[index], axis, s) for s in (2, 1, 3)]
        )
        l_in[index] = l_out[rows_at(index * strip, strip), :]
    share(2)
    second_back = []
    for (first, count), copies, (_, axis, outer, inner, _, _, l_in) in zip(spans, second_copies, orders):
        strip = count // 16
        arrive(copies)
        piece = tri_ref.at[rows_at(half + first + outer * (count // 4) + inner * strip, strip), :]
        piece[...] = l_in[0] + l_in[1] + l_in[2] + l_in[3]
        second_back.append([push(piece, piece, axis, s) for s in (2, 1, 3)])
    share(3)

    def quarter(first, count, index):
        return tri_ref.at[rows_at(half + first + index % 4 * (count // 4), count // 4), :]

    first_back = []
    last_copies = []
    for (first, count), copies, (axis, _, outer, _, _, _, _) in zip(spans, second_back, orders):
        arrive(copies)
        piece = quarter(first, count, outer)
        first_back.append([push(piece, piece, axis, s) for s in (2, 1, 3)])
        last_copies.append(push(piece, piece, "core", 1))
    for (first, count), copies, (_, _, outer, _, _, _, _) in zip(spans, first_back, orders):
        for s, copy in zip((2, 1, 3), copies):
            arrive([copy])
            piece = quarter(first, count, outer - s + 4)
            last_copies.append(push(piece, piece, "core", 1))
    assert used[0] == COPIES
    arrive(last_copies)
    arrive(cols_copies)
    for copy in sent:
        copy.wait_send()


COPIES = 97


def gather(jacobian, residual, bucket, sign_bit, scaling):
    f32 = jnp.float32
    shapes = [
        ((DEV_ROWS, DEV_COLS), jnp.bfloat16),
        ((GROUPS, LANES), f32),
        ((GROUPS, LANES), jnp.int32),
        ((GROUPS, LANES), jnp.int32),
        ((SKETCH, DEV_ROWS), jnp.bfloat16),
        ((SKETCH, LANES), f32),
        ((4, SKETCH, LANES), f32),
        ((4, SKETCH, LANES), f32),
        ((SKETCH, LANES), f32),
        ((4, BLOCK, LANES), f32),
        ((BLOCK, LANES), f32),
        ((4, CHUNK, LANES), f32),
        ((4, RHS_ROWS, LANES), f32),
        ((4, RHS_ROWS, LANES), f32),
        ((4, RHS_ROWS, LANES), f32),
        ((SKETCH, 3 * LANES), jnp.bfloat16),
        ((SKETCH, 3 * LANES), jnp.bfloat16),
        ((TRI_ROWS, LANES), f32),
        ((HALF, LANES), f32),
        ((HALF, LANES), f32),
        ((4, PART_A // 4, LANES), f32),
        ((4, PART_B // 4, LANES), f32),
        ((PART_A // 4, LANES), f32),
        ((PART_B // 4, LANES), f32),
        ((4, PART_A // 16, LANES), f32),
        ((4, PART_B // 16, LANES), f32),
    ]
    return pl.pallas_call(
        functools.partial(gather_kernel, scaling),
        out_shape=(
            jax.ShapeDtypeStruct((TRI_ROWS, LANES), f32),
            jax.ShapeDtypeStruct((RHS_ROWS, LANES), f32),
            jax.ShapeDtypeStruct((4, SKETCH, LANES), f32),
        ),
        in_specs=[pl.BlockSpec(memory_space=pl.ANY)] * 4,
        out_specs=[pl.BlockSpec(memory_space=pltpu.VMEM)] * 3,
        scratch_shapes=[pltpu.VMEM(shape, kind) for shape, kind in shapes]
        + [
            pltpu.SemaphoreType.DMA((4,)),
            pltpu.SemaphoreType.DMA((COPIES,)),
            pltpu.SemaphoreType.DMA((COPIES,)),
        ],
        compiler_params=pltpu.CompilerParams(
            collective_id=0, has_side_effects=True, vmem_limit_bytes=56 * 1024 * 1024
        ),
        name="sketch_and_kernel",
    )(jacobian, residual, bucket, sign_bit)


def total_of(row):
    return jnp.sum(row, axis=(0, 1), keepdims=True)


def solve_kernel(tri_ref, rhs_ref, cols_ref, out_ref, mat, column, answer):
    base = 0
    eye = (
        lax.broadcasted_iota(jnp.int32, (LANES, LANES), 0) == lax.broadcasted_iota(jnp.int32, (LANES, LANES), 1)
    ).astype(jnp.float32) * 0.5
    for i in range(BLOCKS):
        for j in range(i + 1):
            block = tri_ref[base : base + LANES, :] * (1.0 / PARAMS)
            base += LANES
            if i == j:
                block = block + eye
            mat[i * LANES : (i + 1) * LANES, j * LANES : (j + 1) * LANES] = block
            if i != j:
                mat[j * LANES : (j + 1) * LANES, i * LANES : (i + 1) * LANES] = block.T

    raw = jnp.concatenate([rhs_ref[i : i + 1, :] for i in range(BLOCKS)], axis=1)
    largest = jnp.max(jnp.abs(raw), axis=(0, 1), keepdims=True)
    unit = jnp.where(largest > 0, largest, 1.0)
    rhs = raw / unit

    def to_column(row):
        for i in range(BLOCKS):
            piece = jnp.broadcast_to(row[:, i * LANES : (i + 1) * LANES], (LANES, LANES))
            column[i * LANES : (i + 1) * LANES, :] = piece.T

    def product(row):
        to_column(row)
        sums = [jnp.zeros((8, LANES), jnp.float32) for _ in range(BLOCKS)]
        for group in range(SKETCH // 8):
            rows = slice(group * 8, group * 8 + 8)
            weight = column[rows, :]
            for i in range(BLOCKS):
                sums[i] = sums[i] + weight * mat[rows, i * LANES : (i + 1) * LANES]
        return jnp.concatenate([jnp.sum(s, axis=0, keepdims=True) for s in sums], axis=1)

    def met(sol, res, tol):
        scale = total_of(sol * (rhs - res)) - 0.5 * total_of(sol * sol)
        return (tol * tol * scale - 2.0 * total_of(res * res))[0, 0] >= 0.0

    def step(_, carry):
        sol, res, way, size = carry
        image = product(way)
        curve = total_of(way * image)
        alpha = jnp.where(curve > 0, size / curve, 0.0)
        sol = sol + alpha * way
        res = res - alpha * image
        new_size = total_of(res * res)
        beta = jnp.where(size > 0, new_size / size, 0.0)
        return (sol, res, res + beta * way, new_size)

    def round_of(carry):
        count, _, state = carry
        state = lax.fori_loop(0, ROUND_STEPS, step, state)
        return (count + 1, met(state[0], state[1], STOP_TOL), state)

    def go_on(carry):
        count, done, _ = carry
        return jnp.logical_and(count < MAX_ROUNDS, jnp.logical_not(done))

    start = (jnp.zeros_like(rhs), rhs, rhs, total_of(rhs * rhs))
    first_done = largest[0, 0] <= 0.0
    _, _, (sol, _, _, _) = lax.while_loop(go_on, round_of, (0, first_done, start))
    true_res = rhs - product(sol)
    good = met(sol, true_res, ACCEPT_TOL)
    to_column(sol)
    answer[...] = column[...]

    @pl.when(jnp.logical_not(good))
    def _():
        to_column(rhs)
        answer[...] = column[...]
        lanes = lax.broadcasted_iota(jnp.int32, (8, SKETCH), 1)
        below = lax.broadcasted_iota(jnp.int32, (8, LANES), 0)

        def pivot(k, carry):
            pivot_row = mat[pl.ds(k, 1), :]
            pivot_rhs = answer[pl.ds(k, 1), :]
            inverse = 1.0 / jnp.sum(jnp.where(lanes[0:1] == k, pivot_row, 0.0), axis=1, keepdims=True)

            def rows_of(group, inner):
                first = pl.multiple_of(group * 8, 8)
                here = mat[pl.ds(first, 8), :]
                factor = jnp.sum(jnp.where(lanes == k, here, 0.0), axis=1, keepdims=True) * inverse
                factor = jnp.where(below[:, 0:1] + first == k, 0.0, factor)
                mat[pl.ds(first, 8), :] = here - factor * pivot_row
                answer[pl.ds(first, 8), :] = answer[pl.ds(first, 8), :] - factor * pivot_rhs
                return inner

            return lax.fori_loop(0, SKETCH // 8, rows_of, carry)

        lax.fori_loop(0, SKETCH, pivot, 0)

        def divide(group, carry):
            first = pl.multiple_of(group * 8, 8)
            here = mat[pl.ds(first, 8), :]
            row = lax.broadcasted_iota(jnp.int32, (8, SKETCH), 0) + first
            diagonal = jnp.sum(jnp.where(lanes == row, here, 0.0), axis=1, keepdims=True)
            answer[pl.ds(first, 8), :] = answer[pl.ds(first, 8), :] / diagonal
            return carry

        lax.fori_loop(0, SKETCH // 8, divide, 0)

    for lane in range(4):
        values = jnp.sum(answer[...] * cols_ref[lane], axis=0, keepdims=True)
        out_ref[:, lane * LANES : (lane + 1) * LANES] = values * (unit * (1.0 / math.sqrt(PARAMS)))


def solve(tri, rhs, cols):
    return pl.pallas_call(
        solve_kernel,
        out_shape=jax.ShapeDtypeStruct((1, DEV_COLS), jnp.float32),
        in_specs=[pl.BlockSpec(memory_space=pltpu.VMEM)] * 3,
        out_specs=pl.BlockSpec(memory_space=pltpu.VMEM),
        scratch_shapes=[
            pltpu.VMEM((SKETCH, SKETCH), jnp.float32),
            pltpu.VMEM((SKETCH, LANES), jnp.float32),
            pltpu.VMEM((SKETCH, LANES), jnp.float32),
        ],
        compiler_params=pltpu.CompilerParams(vmem_limit_bytes=48 * 1024 * 1024),
        name="solve",
    )(tri, rhs, cols)


def on_device(jacobian, residual, bucket, sign_bit):
    scaling = math.sqrt(SKETCH / (DEV_ROWS * 64))
    tile = (GROUPS, LANES)
    tri, rhs, cols = gather(
        jacobian, residual.reshape(tile), bucket.reshape(tile), sign_bit.reshape(tile), scaling
    )
    update = solve(tri, rhs, cols).reshape(DEV_COLS)
    me = place()
    first = me["near"] * BLOCK + me["far"] * CHUNK + me["x"] * OWN_ROWS
    mine = lax.dynamic_slice_in_dim(cols, first, OWN_ROWS, 1)
    rows = mine.transpose(1, 0, 2).reshape(OWN_ROWS, DEV_COLS)
    return (update, rows)


def solution(mesh):
    return jax.shard_map(
        on_device,
        mesh=mesh,
        in_specs=(P("dp", "col"), P("dp"), P("dp"), P("dp")),
        out_specs=(P("col"), P("dp", "col")),
        check_vma=False,
    )
```

```python
import functools
import math

import jax
import jax.numpy as jnp
from jax import lax
from jax.experimental import pallas as pl
from jax.experimental.pallas import tpu as pltpu
from jax.sharding import PartitionSpec as P

PARAMS = 4096
SKETCH = 768
DEV_ROWS = 2048
DEV_COLS = 512
OWN_ROWS = 12
LANES = 128
CHUNK = 48
BLOCK = 4 * CHUNK
GROUPS = DEV_ROWS // LANES
BLOCKS = SKETCH // LANES
TRI_ROWS = 2816
HALF = TRI_ROWS // 2
PART_A = 640
PART_B = HALF - PART_A
RHS_ROWS = 8
MESH = pl.DeviceIdType.MESH
HIGHEST = lax.Precision.HIGHEST
STOP_TOL = 3e-6
ACCEPT_TOL = 1e-5
ROUND_STEPS = 4
MAX_ROUNDS = 16


def place():
    dp, col = lax.axis_index("dp"), lax.axis_index("col")
    return dict(x=dp % 4, near=(dp // 4) % 4, far=dp // 16, y=col // 2, core=col % 2)


def peer(me, axis, step):
    at = dict(me)
    size = 2 if axis == "core" else 4
    at[axis] = (me[axis] + step) % size
    return (at["far"] * 16 + at["near"] * 4 + at["x"], at["y"] * 2 + at["core"])


def gather_kernel(
    scaling,
    jac_hbm,
    coded_ref,
    res_ref,
    tri_ref,
    rhs_ref,
    cols_ref,
    jac_ref,
    hot,
    acc,
    part,
    x_in,
    x_sum,
    near_in,
    near_sum,
    far_in,
    res_x,
    res_near,
    res_far,
    lhs,
    rhs_t,
    tri,
    core_in,
    k_out,
    k_in_a,
    k_in_b,
    l_out_a,
    l_out_b,
    l_in_a,
    l_in_b,
    load_sem,
    send_sem,
    recv_sem,
):
    me = place()
    x, near, far, y, core = (me[name] for name in ("x", "near", "far", "y", "core"))
    barrier = pltpu.get_barrier_semaphore()
    links = [(axis, step) for axis in ("x", "near", "far", "y") for step in (1, 2, 3)] + [("core", 1)]
    for axis, step in links:
        pl.semaphore_signal(barrier, inc=1, device_id=peer(me, axis, step), device_id_type=MESH)

    load = pltpu.make_async_copy(jac_hbm, jac_ref, load_sem)
    load.start()

    used = [0]
    sent = []

    def push(src, dst, axis, step):
        slot = used[0]
        used[0] += 1
        copy = pltpu.make_async_remote_copy(
            src_ref=src,
            dst_ref=dst,
            send_sem=send_sem.at[slot],
            recv_sem=recv_sem.at[slot],
            device_id=peer(me, axis, step),
            device_id_type=MESH,
        )
        copy.start()
        sent.append(copy)
        return copy

    def arrive(copies):
        for copy in copies:
            copy.wait_recv()

    def rows_at(first, count, unit=8):
        return pl.ds(pl.multiple_of(first, unit), count)

    def block_at(index):
        return rows_at(index % 4 * BLOCK, BLOCK, BLOCK)

    def fill(block, carry):
        chunk = (block % 4) * 4 + block // 4
        targets = (lax.broadcasted_iota(jnp.int32, (CHUNK, LANES), 0) + chunk * CHUNK + 1).astype(jnp.float32)
        first = pl.multiple_of(block * CHUNK, CHUNK)
        total = jnp.zeros((CHUNK, LANES), jnp.float32)
        for group in range(GROUPS):
            code = coded_ref[group : group + 1, :]
            hit = jnp.abs(code) == targets
            total = total + jnp.where(hit, res_ref[group : group + 1, :], 0.0)
            signed = jnp.where(hit, jnp.where(code > 0.0, 1.0, -1.0), 0.0)
            hot[pl.ds(first, CHUNK), group * LANES : (group + 1) * LANES] = signed.astype(jnp.bfloat16)
        acc[pl.ds(first, CHUNK), :] = total
        return carry

    lax.fori_loop(0, SKETCH // CHUNK, fill, 0)
    load.wait()

    x_copies = []
    for q in range(4):
        rows = block_at(near + 1 + q)
        terms = jnp.dot(hot[rows, :], jac_ref[...], preferred_element_type=jnp.float32)
        for lane in range(4):
            part[lane, rows, :] = terms[:, lane * LANES : (lane + 1) * LANES]
        if q == 0:
            pl.semaphore_wait(barrier, len(links))
        x_copies.append([push(part.at[(x + s) % 4, rows, :], x_in.at[x, rows, :], "x", s) for s in (2, 1, 3)])

    res_row = lax.dot_general(
        jnp.ones((RHS_ROWS, LANES), jnp.float32),
        acc[...],
        (((1,), (1,)), ((), ())),
        precision=HIGHEST,
        preferred_element_type=jnp.float32,
    )
    res_x[x] = jnp.concatenate(
        [res_row[0:1, i * LANES : (i + 1) * LANES] for i in range(BLOCKS)]
        + [jnp.zeros((RHS_ROWS - BLOCKS, LANES), jnp.float32)],
        axis=0,
    )
    res_copies = [push(res_x.at[x], res_x.at[x], "x", s) for s in (1, 2, 3)]

    near_copies = []
    for q in range(4):
        rows = block_at(near + 1 + q)
        arrive(x_copies[q])
        summed = part[x, rows, :]
        for s in (1, 2, 3):
            summed = summed + x_in[(x + s) % 4, rows, :]
        if q < 3:
            x_sum[rows, :] = summed
            near_copies.append(push(x_sum.at[rows, :], near_in.at[near], "near", q + 1))
        else:
            near_in[near] = summed
        if q == 1:
            arrive(res_copies)
            res_near[near] = res_x[0] + res_x[1] + res_x[2] + res_x[3]
            res_copies = [push(res_near.at[near], res_near.at[near], "near", s) for s in (1, 2, 3)]
    arrive(near_copies)
    near_sum[...] = near_in[0] + near_in[1] + near_in[2] + near_in[3]

    far_copies = []
    for s in (2, 1, 3):
        rows = rows_at((far + s) % 4 * CHUNK, CHUNK, CHUNK)
        far_copies.append(push(near_sum.at[rows, :], far_in.at[far], "far", s))
    far_in[far] = near_sum[rows_at(far * CHUNK, CHUNK, CHUNK), :]
    arrive(res_copies)
    res_far[far] = res_near[0] + res_near[1] + res_near[2] + res_near[3]
    res_copies = [push(res_far.at[far], res_far.at[far], "far", s) for s in (1, 2, 3)]
    arrive(far_copies)

    def chunk_of(at_near, at_far):
        rows = rows_at(at_near % 4 * BLOCK + at_far % 4 * CHUNK, CHUNK, CHUNK)
        return cols_ref.at[x, rows, :]

    own = chunk_of(near, far)
    own[...] = (far_in[0] + far_in[1] + far_in[2] + far_in[3]) * scaling

    far_copies = {s: push(own, own, "far", s) for s in (2, 1, 3)}
    near_copies = [push(own, own, "near", s) for s in (2, 1, 3)]
    cols_copies = [push(own, own, "x", s) for s in (2, 1, 3)]
    arrive(res_copies)
    rhs_ref[...] = (res_far[0] + res_far[1] + res_far[2] + res_far[3]) * scaling
    for s in (1, 3, 2):
        arrive([far_copies[s]])
        chunk = chunk_of(near, far - s + 4)
        near_copies += [push(chunk, chunk, "near", t) for t in (2, 1, 3)]
        cols_copies += [push(chunk, chunk, "x", t) for t in (2, 1, 3)]
    arrive(near_copies)

    def share(step):
        block = cols_ref.at[x, block_at(near + step), :]
        cols_copies.extend([push(block, block, "x", t) for t in (2, 1, 3)])

    share(1)

    values = cols_ref[x]
    high = values.astype(jnp.bfloat16)
    low = (values - high.astype(jnp.float32)).astype(jnp.bfloat16)
    lhs[:, 0:LANES] = high
    lhs[:, LANES : 2 * LANES] = high
    lhs[:, 2 * LANES :] = low
    rhs_t[:, 0:LANES] = high
    rhs_t[:, LANES : 2 * LANES] = low
    rhs_t[:, 2 * LANES :] = high
    base = 0
    for i in range(BLOCKS):
        width = (i + 1) * LANES
        product = lax.dot_general(
            lhs[i * LANES : width, :],
            rhs_t[0:width, :],
            (((1,), (1,)), ((), ())),
            preferred_element_type=jnp.float32,
        )
        for j in range(i + 1):
            tri[base : base + LANES, :] = product[:, j * LANES : (j + 1) * LANES]
            base += LANES
    tri[base:, :] = jnp.zeros((TRI_ROWS - base, LANES), jnp.float32)

    half = core * HALF
    other = (1 - core) * HALF
    spans = ((0, PART_A), (PART_A, PART_B))
    core_copies = [
        push(tri.at[rows_at(other + first, count), :], core_in.at[first : first + count, :], "core", 1)
        for first, count in spans
    ]
    orders = (("x", "y", x, y, k_in_a, l_out_a, l_in_a), ("y", "x", y, x, k_in_b, l_out_b, l_in_b))

    first_copies = []
    for (first, count), copy, (axis, _, index, _, k_in, _, _) in zip(spans, core_copies, orders):
        arrive([copy])
        k_out[first : first + count, :] = tri[rows_at(half + first, count), :] + core_in[first : first + count, :]
        strip = count // 4
        first_copies.append(
            [
                push(k_out.at[rows_at(first + (index + s) % 4 * strip, strip), :], k_in.at[index], axis, s)
                for s in (2, 1, 3)
            ]
        )
        k_in[index] = k_out[rows_at(first + index * strip, strip), :]
    second_copies = []
    for (first, count), copies, (_, axis, _, index, k_in, l_out, l_in) in zip(spans, first_copies, orders):
        strip = count // 16
        arrive(copies)
        l_out[...] = k_in[0] + k_in[1] + k_in[2] + k_in[3]
        second_copies.append(
            [push(l_out.at[rows_at((index + s) % 4 * strip, strip), :], l_in.at[index], axis, s) for s in (2, 1, 3)]
        )
        l_in[index] = l_out[rows_at(index * strip, strip), :]
    share(2)
    second_back = []
    for (first, count), copies, (_, axis, outer, inner, _, _, l_in) in zip(spans, second_copies, orders):
        strip = count // 16
        arrive(copies)
        piece = tri_ref.at[rows_at(half + first + outer * (count // 4) + inner * strip, strip), :]
        piece[...] = l_in[0] + l_in[1] + l_in[2] + l_in[3]
        second_back.append([push(piece, piece, axis, s) for s in (2, 1, 3)])
    share(3)

    def quarter(first, count, index):
        return tri_ref.at[rows_at(half + first + index % 4 * (count // 4), count // 4), :]

    first_back = []
    last_copies = []
    for (first, count), copies, (axis, _, outer, _, _, _, _) in zip(spans, second_back, orders):
        arrive(copies)
        piece = quarter(first, count, outer)
        first_back.append([push(piece, piece, axis, s) for s in (2, 1, 3)])
        last_copies.append(push(piece, piece, "core", 1))
    for (first, count), copies, (_, _, outer, _, _, _, _) in zip(spans, first_back, orders):
        for s, copy in zip((2, 1, 3), copies):
            arrive([copy])
            piece = quarter(first, count, outer - s + 4)
            last_copies.append(push(piece, piece, "core", 1))
    assert used[0] == COPIES
    arrive(last_copies)
    arrive(cols_copies)
    for copy in sent:
        copy.wait_send()


COPIES = 97


def gather(jacobian, coded, residual, scaling):
    f32 = jnp.float32
    shapes = [
        ((DEV_ROWS, DEV_COLS), jnp.bfloat16),
        ((SKETCH, DEV_ROWS), jnp.bfloat16),
        ((SKETCH, LANES), f32),
        ((4, SKETCH, LANES), f32),
        ((4, SKETCH, LANES), f32),
        ((SKETCH, LANES), f32),
        ((4, BLOCK, LANES), f32),
        ((BLOCK, LANES), f32),
        ((4, CHUNK, LANES), f32),
        ((4, RHS_ROWS, LANES), f32),
        ((4, RHS_ROWS, LANES), f32),
        ((4, RHS_ROWS, LANES), f32),
        ((SKETCH, 3 * LANES), jnp.bfloat16),
        ((SKETCH, 3 * LANES), jnp.bfloat16),
        ((TRI_ROWS, LANES), f32),
        ((HALF, LANES), f32),
        ((HALF, LANES), f32),
        ((4, PART_A // 4, LANES), f32),
        ((4, PART_B // 4, LANES), f32),
        ((PART_A // 4, LANES), f32),
        ((PART_B // 4, LANES), f32),
        ((4, PART_A // 16, LANES), f32),
        ((4, PART_B // 16, LANES), f32),
    ]
    return pl.pallas_call(
        functools.partial(gather_kernel, scaling),
        out_shape=(
            jax.ShapeDtypeStruct((TRI_ROWS, LANES), f32),
            jax.ShapeDtypeStruct((RHS_ROWS, LANES), f32),
            jax.ShapeDtypeStruct((4, SKETCH, LANES), f32),
        ),
        in_specs=[pl.BlockSpec(memory_space=pl.ANY), pl.BlockSpec(memory_space=pltpu.VMEM), pl.BlockSpec(memory_space=pltpu.VMEM)],
        out_specs=[pl.BlockSpec(memory_space=pltpu.VMEM)] * 3,
        scratch_shapes=[pltpu.VMEM(shape, kind) for shape, kind in shapes]
        + [
            pltpu.SemaphoreType.DMA,
            pltpu.SemaphoreType.DMA((COPIES,)),
            pltpu.SemaphoreType.DMA((COPIES,)),
        ],
        compiler_params=pltpu.CompilerParams(
            collective_id=0, has_side_effects=True, vmem_limit_bytes=50 * 1024 * 1024
        ),
        name="sketch_and_kernel",
    )(jacobian, coded, residual)


def total_of(row):
    return jnp.sum(row, axis=(0, 1), keepdims=True)


def solve_kernel(tri_ref, rhs_ref, cols_ref, out_ref, rows_ref, mat, column, answer):
    me = place()
    first = pl.multiple_of(me["near"] * BLOCK + me["far"] * CHUNK, CHUNK)
    for lane in range(4):
        chunk = cols_ref[lane, pl.ds(first, CHUNK), :]
        mine = chunk[:OWN_ROWS]
        for i in range(1, 4):
            mine = jnp.where(me["x"] == i, chunk[i * OWN_ROWS : (i + 1) * OWN_ROWS], mine)
        rows_ref[:, lane * LANES : (lane + 1) * LANES] = mine

    base = 0
    eye = (
        lax.broadcasted_iota(jnp.int32, (LANES, LANES), 0) == lax.broadcasted_iota(jnp.int32, (LANES, LANES), 1)
    ).astype(jnp.float32) * 0.5
    for i in range(BLOCKS):
        for j in range(i + 1):
            block = tri_ref[base : base + LANES, :] * (1.0 / PARAMS)
            base += LANES
            if i == j:
                block = block + eye
            mat[i * LANES : (i + 1) * LANES, j * LANES : (j + 1) * LANES] = block
            if i != j:
                mat[j * LANES : (j + 1) * LANES, i * LANES : (i + 1) * LANES] = block.T

    raw = jnp.concatenate([rhs_ref[i : i + 1, :] for i in range(BLOCKS)], axis=1)
    largest = jnp.max(jnp.abs(raw), axis=(0, 1), keepdims=True)
    unit = jnp.where(largest > 0, largest, 1.0)
    rhs = raw / unit

    def to_column(row):
        for i in range(BLOCKS):
            piece = jnp.broadcast_to(row[:, i * LANES : (i + 1) * LANES], (LANES, LANES))
            column[i * LANES : (i + 1) * LANES, :] = piece.T

    def product(row):
        to_column(row)
        sums = [jnp.zeros((8, LANES), jnp.float32) for _ in range(BLOCKS)]
        for group in range(SKETCH // 8):
            rows = slice(group * 8, group * 8 + 8)
            weight = column[rows, :]
            for i in range(BLOCKS):
                sums[i] = sums[i] + weight * mat[rows, i * LANES : (i + 1) * LANES]
        return jnp.concatenate([jnp.sum(s, axis=0, keepdims=True) for s in sums], axis=1)

    def met(sol, res, tol):
        scale = total_of(sol * (rhs - res)) - 0.5 * total_of(sol * sol)
        return (tol * tol * scale - 2.0 * total_of(res * res))[0, 0] >= 0.0

    def step(_, carry):
        sol, res, way, size = carry
        image = product(way)
        curve = total_of(way * image)
        alpha = jnp.where(curve > 0, size / curve, 0.0)
        sol = sol + alpha * way
        res = res - alpha * image
        new_size = total_of(res * res)
        beta = jnp.where(size > 0, new_size / size, 0.0)
        return (sol, res, res + beta * way, new_size)

    def round_of(carry):
        count, _, state = carry
        state = lax.fori_loop(0, ROUND_STEPS, step, state)
        return (count + 1, met(state[0], state[1], STOP_TOL), state)

    def go_on(carry):
        count, done, _ = carry
        return jnp.logical_and(count < MAX_ROUNDS, jnp.logical_not(done))

    start = (jnp.zeros_like(rhs), rhs, rhs, total_of(rhs * rhs))
    first_done = largest[0, 0] <= 0.0
    _, _, (sol, _, _, _) = lax.while_loop(go_on, round_of, (0, first_done, start))
    true_res = rhs - product(sol)
    good = met(sol, true_res, ACCEPT_TOL)
    to_column(sol)
    answer[...] = column[...]

    @pl.when(jnp.logical_not(good))
    def _():
        to_column(rhs)
        answer[...] = column[...]
        lanes = lax.broadcasted_iota(jnp.int32, (8, SKETCH), 1)
        below = lax.broadcasted_iota(jnp.int32, (8, LANES), 0)

        def pivot(k, carry):
            pivot_row = mat[pl.ds(k, 1), :]
            pivot_rhs = answer[pl.ds(k, 1), :]
            inverse = 1.0 / jnp.sum(jnp.where(lanes[0:1] == k, pivot_row, 0.0), axis=1, keepdims=True)

            def rows_of(group, inner):
                first = pl.multiple_of(group * 8, 8)
                here = mat[pl.ds(first, 8), :]
                factor = jnp.sum(jnp.where(lanes == k, here, 0.0), axis=1, keepdims=True) * inverse
                factor = jnp.where(below[:, 0:1] + first == k, 0.0, factor)
                mat[pl.ds(first, 8), :] = here - factor * pivot_row
                answer[pl.ds(first, 8), :] = answer[pl.ds(first, 8), :] - factor * pivot_rhs
                return inner

            return lax.fori_loop(0, SKETCH // 8, rows_of, carry)

        lax.fori_loop(0, SKETCH, pivot, 0)

        def divide(group, carry):
            first = pl.multiple_of(group * 8, 8)
            here = mat[pl.ds(first, 8), :]
            row = lax.broadcasted_iota(jnp.int32, (8, SKETCH), 0) + first
            diagonal = jnp.sum(jnp.where(lanes == row, here, 0.0), axis=1, keepdims=True)
            answer[pl.ds(first, 8), :] = answer[pl.ds(first, 8), :] / diagonal
            return carry

        lax.fori_loop(0, SKETCH // 8, divide, 0)

    for lane in range(4):
        values = jnp.sum(answer[...] * cols_ref[lane], axis=0, keepdims=True)
        out_ref[:, lane * LANES : (lane + 1) * LANES] = values * (unit * (1.0 / math.sqrt(PARAMS)))


def solve(tri, rhs, cols):
    return pl.pallas_call(
        solve_kernel,
        out_shape=(
            jax.ShapeDtypeStruct((1, DEV_COLS), jnp.float32),
            jax.ShapeDtypeStruct((OWN_ROWS, DEV_COLS), jnp.float32),
        ),
        in_specs=[pl.BlockSpec(memory_space=pltpu.VMEM)] * 3,
        out_specs=[pl.BlockSpec(memory_space=pltpu.VMEM)] * 2,
        scratch_shapes=[
            pltpu.VMEM((SKETCH, SKETCH), jnp.float32),
            pltpu.VMEM((SKETCH, LANES), jnp.float32),
            pltpu.VMEM((SKETCH, LANES), jnp.float32),
        ],
        compiler_params=pltpu.CompilerParams(vmem_limit_bytes=16 * 1024 * 1024),
        name="solve",
    )(tri, rhs, cols)


def on_device(jacobian, residual, bucket, sign_bit):
    scaling = math.sqrt(SKETCH / (DEV_ROWS * 64))
    tile = (GROUPS, LANES)
    signs = (2 * sign_bit - 1).astype(jnp.float32)
    coded = (bucket.astype(jnp.float32) + 1.0) * signs
    tri, rhs, cols = gather(jacobian, coded.reshape(tile), (residual * signs).reshape(tile), scaling)
    update, rows = solve(tri, rhs, cols)
    return (update.reshape(DEV_COLS), rows)


def solution(mesh):
    return jax.shard_map(
        on_device,
        mesh=mesh,
        in_specs=(P("dp", "col"), P("dp"), P("dp"), P("dp")),
        out_specs=(P("col"), P("dp", "col")),
        check_vma=False,
    )
```

```python
import functools
import math

import jax
import jax.numpy as jnp
from jax import lax
from jax.experimental import pallas as pl
from jax.experimental.pallas import tpu as pltpu
from jax.sharding import PartitionSpec as P

PARAMS = 4096
SKETCH = 768
DEV_ROWS = 2048
DEV_COLS = 512
OWN_ROWS = 12
LANES = 128
CHUNK = 48
BLOCK = 4 * CHUNK
GROUPS = DEV_ROWS // LANES
BLOCKS = SKETCH // LANES
TRI_ROWS = 2816
HALF = TRI_ROWS // 2
PART_A = 640
PART_B = HALF - PART_A
RHS_ROWS = 8
MESH = pl.DeviceIdType.MESH
HIGHEST = lax.Precision.HIGHEST
STOP_TOL = 3e-6
ACCEPT_TOL = 1e-5
ROUND_STEPS = 4
MAX_ROUNDS = 16


def place():
    dp, col = lax.axis_index("dp"), lax.axis_index("col")
    return dict(x=dp % 4, near=(dp // 4) % 4, far=dp // 16, y=col // 2, core=col % 2)


def peer(me, axis, step):
    at = dict(me)
    size = 2 if axis == "core" else 4
    at[axis] = (me[axis] + step) % size
    return (at["far"] * 16 + at["near"] * 4 + at["x"], at["y"] * 2 + at["core"])


def along_z(me, step):
    z = (me["far"] * 4 + me["near"] + step + 16) % 16
    return (z * 4 + me["x"], me["y"] * 2 + me["core"])


def gather_kernel(
    scaling,
    jac_hbm,
    coded_ref,
    res_ref,
    tri_ref,
    rhs_ref,
    cols_ref,
    jac_ref,
    hot,
    acc,
    part,
    fold_in,
    x_in,
    x_sum,
    near_in,
    near_sum,
    far_in,
    res_x,
    res_near,
    res_far,
    lhs,
    rhs_t,
    tri,
    core_in,
    k_out,
    k_in_a,
    k_in_b,
    l_out_a,
    l_out_b,
    l_in_a,
    l_in_b,
    known_sem,
    load_sem,
    send_sem,
    recv_sem,
):
    me = place()
    x, near, far, y, core = (me[name] for name in ("x", "near", "far", "y", "core"))
    barrier = pltpu.get_barrier_semaphore()
    beside = [peer(me, axis, step) for axis, step in (("x", 1), ("x", 3), ("y", 1), ("y", 3), ("core", 1))]
    beside += [along_z(me, 1), along_z(me, -1)]
    for device in beside:
        pl.semaphore_signal(barrier, inc=1, device_id=device, device_id_type=MESH)

    def vouch(level, devices):
        for device in devices:
            pl.semaphore_signal(known_sem.at[level], inc=1, device_id=device, device_id_type=MESH)

    load = pltpu.make_async_copy(jac_hbm, jac_ref, load_sem)
    load.start()

    used = [0]
    sent = []

    def push(src, dst, axis, step):
        slot = used[0]
        used[0] += 1
        copy = pltpu.make_async_remote_copy(
            src_ref=src,
            dst_ref=dst,
            send_sem=send_sem.at[slot],
            recv_sem=recv_sem.at[slot],
            device_id=peer(me, axis, step),
            device_id_type=MESH,
        )
        copy.start()
        sent.append(copy)
        return copy

    def arrive(copies):
        for copy in copies:
            copy.wait_recv()

    def rows_at(first, count, unit=8):
        return pl.ds(pl.multiple_of(first, unit), count)

    def block_at(index):
        return rows_at(index % 4 * BLOCK, BLOCK, BLOCK)

    def half_of(rows, side):
        return rows_at(rows.start + side * (BLOCK // 2), BLOCK // 2, BLOCK // 2)

    def fill(block, carry):
        chunk = (block % 4) * 4 + block // 4
        targets = (lax.broadcasted_iota(jnp.int32, (CHUNK, LANES), 0) + chunk * CHUNK + 1).astype(jnp.float32)
        first = pl.multiple_of(block * CHUNK, CHUNK)
        total = jnp.zeros((CHUNK, LANES), jnp.float32)
        for group in range(GROUPS):
            code = coded_ref[group : group + 1, :]
            hit = jnp.abs(code) == targets
            total = total + jnp.where(hit, res_ref[group : group + 1, :], 0.0)
            signed = jnp.where(hit, jnp.where(code > 0.0, 1.0, -1.0), 0.0)
            hot[pl.ds(first, CHUNK), group * LANES : (group + 1) * LANES] = signed.astype(jnp.bfloat16)
        acc[pl.ds(first, CHUNK), :] = total
        return carry

    lax.fori_loop(0, SKETCH // CHUNK, fill, 0)
    load.wait()

    fold_copies = []
    for q in range(4):
        rows = block_at(near + 1 + q)
        terms = jnp.dot(hot[rows, :], jac_ref[...], preferred_element_type=jnp.float32)
        for lane in range(4):
            part[lane, rows, :] = terms[:, lane * LANES : (lane + 1) * LANES]
        if q == 0:
            pl.semaphore_wait(barrier, len(beside))
            vouch(0, [peer(me, "x", 3), peer(me, "y", 3), along_z(me, 1), along_z(me, -1)])
        two_away = (x + 2) % 4
        fold_copies.append(
            [
                push(part.at[two_away, half_of(rows, 0), :], fold_in.at[0, half_of(rows, 0), :], "x", 1),
                push(part.at[two_away, half_of(rows, 1), :], fold_in.at[1, half_of(rows, 1), :], "x", 3),
            ]
        )
    pl.semaphore_wait(known_sem.at[0], 4)
    vouch(1, [along_z(me, 2), along_z(me, -2)])

    res_row = lax.dot_general(
        jnp.ones((RHS_ROWS, LANES), jnp.float32),
        acc[...],
        (((1,), (1,)), ((), ())),
        precision=HIGHEST,
        preferred_element_type=jnp.float32,
    )
    res_x[x] = jnp.concatenate(
        [res_row[0:1, i * LANES : (i + 1) * LANES] for i in range(BLOCKS)]
        + [jnp.zeros((RHS_ROWS - BLOCKS, LANES), jnp.float32)],
        axis=0,
    )
    res_copies = [push(res_x.at[x], res_x.at[x], "x", s) for s in (1, 2, 3)]

    x_copies = []
    for q in range(4):
        rows = block_at(near + 1 + q)
        arrive(fold_copies[q])
        for step, side in ((1, 0), (3, 1)):
            index = (x + step) % 4
            there = half_of(rows, side)
            part[index, there, :] = part[index, there, :] + fold_in[side, there, :]
        x_copies.append(
            [push(part.at[(x + s) % 4, rows, :], x_in.at[side, rows, :], "x", s) for s, side in ((1, 0), (3, 1))]
        )
    pl.semaphore_wait(known_sem.at[1], 2)
    vouch(2, [along_z(me, 4), along_z(me, -4)])

    near_copies = []
    for q in range(4):
        rows = block_at(near + 1 + q)
        arrive(x_copies[q])
        summed = part[x, rows, :] + x_in[0, rows, :] + x_in[1, rows, :]
        if q < 3:
            x_sum[rows, :] = summed
            near_copies.append(push(x_sum.at[rows, :], near_in.at[near], "near", q + 1))
        else:
            near_in[near] = summed
        if q == 1:
            arrive(res_copies)
            res_near[near] = res_x[0] + res_x[1] + res_x[2] + res_x[3]
            res_copies = [push(res_near.at[near], res_near.at[near], "near", s) for s in (1, 2, 3)]
    arrive(near_copies)
    near_sum[...] = near_in[0] + near_in[1] + near_in[2] + near_in[3]

    pl.semaphore_wait(known_sem.at[2], 2)
    far_copies = []
    for s in (2, 1, 3):
        rows = rows_at((far + s) % 4 * CHUNK, CHUNK, CHUNK)
        far_copies.append(push(near_sum.at[rows, :], far_in.at[far], "far", s))
    far_in[far] = near_sum[rows_at(far * CHUNK, CHUNK, CHUNK), :]
    arrive(res_copies)
    res_far[far] = res_near[0] + res_near[1] + res_near[2] + res_near[3]
    res_copies = [push(res_far.at[far], res_far.at[far], "far", s) for s in (1, 2, 3)]
    arrive(far_copies)

    def chunk_of(at_near, at_far):
        rows = rows_at(at_near % 4 * BLOCK + at_far % 4 * CHUNK, CHUNK, CHUNK)
        return cols_ref.at[x, rows, :]

    own = chunk_of(near, far)
    own[...] = (far_in[0] + far_in[1] + far_in[2] + far_in[3]) * scaling

    far_copies = {s: push(own, own, "far", s) for s in (2, 1, 3)}
    near_copies = [push(own, own, "near", s) for s in (2, 1, 3)]
    cols_copies = [[push(own, own, "x", s) for s in (1, 3)], [], [], []]
    arrive(res_copies)
    rhs_ref[...] = (res_far[0] + res_far[1] + res_far[2] + res_far[3]) * scaling
    for s in (1, 3, 2):
        arrive([far_copies[s]])
        chunk = chunk_of(near, far - s + 4)
        near_copies += [push(chunk, chunk, "near", t) for t in (2, 1, 3)]
        cols_copies[0] += [push(chunk, chunk, "x", t) for t in (1, 3)]
    arrive(near_copies)

    def share(step):
        block = cols_ref.at[x, block_at(near + step), :]
        cols_copies[step] += [push(block, block, "x", t) for t in (1, 3)]

    def share_on(step):
        arrive(cols_copies[step])
        for t, side in ((1, 0), (3, 1)):
            there = cols_ref.at[(x - t + 4) % 4, half_of(block_at(near + step), side), :]
            on_copies.append(push(there, there, "x", t))

    on_copies = []
    share_on(0)
    share(1)

    values = cols_ref[x]
    high = values.astype(jnp.bfloat16)
    low = (values - high.astype(jnp.float32)).astype(jnp.bfloat16)
    lhs[:, 0:LANES] = high
    lhs[:, LANES : 2 * LANES] = high
    lhs[:, 2 * LANES :] = low
    rhs_t[:, 0:LANES] = high
    rhs_t[:, LANES : 2 * LANES] = low
    rhs_t[:, 2 * LANES :] = high
    base = 0
    for i in range(BLOCKS):
        width = (i + 1) * LANES
        product = lax.dot_general(
            lhs[i * LANES : width, :],
            rhs_t[0:width, :],
            (((1,), (1,)), ((), ())),
            preferred_element_type=jnp.float32,
        )
        for j in range(i + 1):
            tri[base : base + LANES, :] = product[:, j * LANES : (j + 1) * LANES]
            base += LANES
    tri[base:, :] = jnp.zeros((TRI_ROWS - base, LANES), jnp.float32)

    half = core * HALF
    other = (1 - core) * HALF
    spans = ((0, PART_A), (PART_A, PART_B))
    core_copies = [
        push(tri.at[rows_at(other + first, count), :], core_in.at[first : first + count, :], "core", 1)
        for first, count in spans
    ]
    orders = (("x", "y", x, y, k_in_a, l_out_a, l_in_a), ("y", "x", y, x, k_in_b, l_out_b, l_in_b))

    first_copies = []
    for (first, count), copy, (axis, _, index, _, k_in, _, _) in zip(spans, core_copies, orders):
        arrive([copy])
        k_out[first : first + count, :] = tri[rows_at(half + first, count), :] + core_in[first : first + count, :]
        strip = count // 4
        first_copies.append(
            [
                push(k_out.at[rows_at(first + (index + s) % 4 * strip, strip), :], k_in.at[index], axis, s)
                for s in (2, 1, 3)
            ]
        )
        k_in[index] = k_out[rows_at(first + index * strip, strip), :]
    second_copies = []
    for (first, count), copies, (_, axis, _, index, k_in, l_out, l_in) in zip(spans, first_copies, orders):
        strip = count // 16
        arrive(copies)
        l_out[...] = k_in[0] + k_in[1] + k_in[2] + k_in[3]
        second_copies.append(
            [push(l_out.at[rows_at((index + s) % 4 * strip, strip), :], l_in.at[index], axis, s) for s in (2, 1, 3)]
        )
        l_in[index] = l_out[rows_at(index * strip, strip), :]
    share_on(1)
    share(2)
    second_back = []
    for (first, count), copies, (_, axis, outer, inner, _, _, l_in) in zip(spans, second_copies, orders):
        strip = count // 16
        arrive(copies)
        piece = tri_ref.at[rows_at(half + first + outer * (count // 4) + inner * strip, strip), :]
        piece[...] = l_in[0] + l_in[1] + l_in[2] + l_in[3]
        second_back.append([push(piece, piece, axis, s) for s in (2, 1, 3)])
    share_on(2)
    share(3)

    def quarter(first, count, index):
        return tri_ref.at[rows_at(half + first + index % 4 * (count // 4), count // 4), :]

    first_back = []
    last_copies = []
    for (first, count), copies, (axis, _, outer, _, _, _, _) in zip(spans, second_back, orders):
        arrive(copies)
        piece = quarter(first, count, outer)
        first_back.append([push(piece, piece, axis, s) for s in (2, 1, 3)])
        last_copies.append(push(piece, piece, "core", 1))
    share_on(3)
    for (first, count), copies, (_, _, outer, _, _, _, _) in zip(spans, first_back, orders):
        for s, copy in zip((2, 1, 3), copies):
            arrive([copy])
            piece = quarter(first, count, outer - s + 4)
            last_copies.append(push(piece, piece, "core", 1))
    assert used[0] == COPIES
    arrive(last_copies)
    arrive(on_copies)
    for copy in sent:
        copy.wait_send()


COPIES = 102


def gather(jacobian, coded, residual, scaling):
    f32 = jnp.float32
    shapes = [
        ((DEV_ROWS, DEV_COLS), jnp.bfloat16),
        ((SKETCH, DEV_ROWS), jnp.bfloat16),
        ((SKETCH, LANES), f32),
        ((4, SKETCH, LANES), f32),
        ((2, SKETCH, LANES), f32),
        ((2, SKETCH, LANES), f32),
        ((SKETCH, LANES), f32),
        ((4, BLOCK, LANES), f32),
        ((BLOCK, LANES), f32),
        ((4, CHUNK, LANES), f32),
        ((4, RHS_ROWS, LANES), f32),
        ((4, RHS_ROWS, LANES), f32),
        ((4, RHS_ROWS, LANES), f32),
        ((SKETCH, 3 * LANES), jnp.bfloat16),
        ((SKETCH, 3 * LANES), jnp.bfloat16),
        ((TRI_ROWS, LANES), f32),
        ((HALF, LANES), f32),
        ((HALF, LANES), f32),
        ((4, PART_A // 4, LANES), f32),
        ((4, PART_B // 4, LANES), f32),
        ((PART_A // 4, LANES), f32),
        ((PART_B // 4, LANES), f32),
        ((4, PART_A // 16, LANES), f32),
        ((4, PART_B // 16, LANES), f32),
    ]
    return pl.pallas_call(
        functools.partial(gather_kernel, scaling),
        out_shape=(
            jax.ShapeDtypeStruct((TRI_ROWS, LANES), f32),
            jax.ShapeDtypeStruct((RHS_ROWS, LANES), f32),
            jax.ShapeDtypeStruct((4, SKETCH, LANES), f32),
        ),
        in_specs=[pl.BlockSpec(memory_space=pl.ANY), pl.BlockSpec(memory_space=pltpu.VMEM), pl.BlockSpec(memory_space=pltpu.VMEM)],
        out_specs=[pl.BlockSpec(memory_space=pltpu.VMEM)] * 3,
        scratch_shapes=[pltpu.VMEM(shape, kind) for shape, kind in shapes]
        + [
            pltpu.SemaphoreType.REGULAR((3,)),
            pltpu.SemaphoreType.DMA,
            pltpu.SemaphoreType.DMA((COPIES,)),
            pltpu.SemaphoreType.DMA((COPIES,)),
        ],
        compiler_params=pltpu.CompilerParams(
            collective_id=0, has_side_effects=True, vmem_limit_bytes=50 * 1024 * 1024
        ),
        name="sketch_and_kernel",
    )(jacobian, coded, residual)


def total_of(row):
    return jnp.sum(row, axis=(0, 1), keepdims=True)


def solve_kernel(tri_ref, rhs_ref, cols_ref, out_ref, rows_ref, mat, column, answer):
    me = place()
    first = pl.multiple_of(me["near"] * BLOCK + me["far"] * CHUNK, CHUNK)
    for lane in range(4):
        chunk = cols_ref[lane, pl.ds(first, CHUNK), :]
        mine = chunk[:OWN_ROWS]
        for i in range(1, 4):
            mine = jnp.where(me["x"] == i, chunk[i * OWN_ROWS : (i + 1) * OWN_ROWS], mine)
        rows_ref[:, lane * LANES : (lane + 1) * LANES] = mine

    base = 0
    eye = (
        lax.broadcasted_iota(jnp.int32, (LANES, LANES), 0) == lax.broadcasted_iota(jnp.int32, (LANES, LANES), 1)
    ).astype(jnp.float32) * 0.5
    for i in range(BLOCKS):
        for j in range(i + 1):
            block = tri_ref[base : base + LANES, :] * (1.0 / PARAMS)
            base += LANES
            if i == j:
                block = block + eye
            mat[i * LANES : (i + 1) * LANES, j * LANES : (j + 1) * LANES] = block
            if i != j:
                mat[j * LANES : (j + 1) * LANES, i * LANES : (i + 1) * LANES] = block.T

    raw = jnp.concatenate([rhs_ref[i : i + 1, :] for i in range(BLOCKS)], axis=1)
    largest = jnp.max(jnp.abs(raw), axis=(0, 1), keepdims=True)
    unit = jnp.where(largest > 0, largest, 1.0)
    rhs = raw / unit

    def to_column(row):
        for i in range(BLOCKS):
            piece = jnp.broadcast_to(row[:, i * LANES : (i + 1) * LANES], (LANES, LANES))
            column[i * LANES : (i + 1) * LANES, :] = piece.T

    def product(row):
        to_column(row)
        sums = [jnp.zeros((8, LANES), jnp.float32) for _ in range(BLOCKS)]
        for group in range(SKETCH // 8):
            rows = slice(group * 8, group * 8 + 8)
            weight = column[rows, :]
            for i in range(BLOCKS):
                sums[i] = sums[i] + weight * mat[rows, i * LANES : (i + 1) * LANES]
        return jnp.concatenate([jnp.sum(s, axis=0, keepdims=True) for s in sums], axis=1)

    def met(sol, res, tol):
        scale = total_of(sol * (rhs - res)) - 0.5 * total_of(sol * sol)
        return (tol * tol * scale - 2.0 * total_of(res * res))[0, 0] >= 0.0

    def step(_, carry):
        sol, res, way, size = carry
        image = product(way)
        curve = total_of(way * image)
        alpha = jnp.where(curve > 0, size / curve, 0.0)
        sol = sol + alpha * way
        res = res - alpha * image
        new_size = total_of(res * res)
        beta = jnp.where(size > 0, new_size / size, 0.0)
        return (sol, res, res + beta * way, new_size)

    def round_of(carry):
        count, _, state = carry
        state = lax.fori_loop(0, ROUND_STEPS, step, state)
        return (count + 1, met(state[0], state[1], STOP_TOL), state)

    def go_on(carry):
        count, done, _ = carry
        return jnp.logical_and(count < MAX_ROUNDS, jnp.logical_not(done))

    start = (jnp.zeros_like(rhs), rhs, rhs, total_of(rhs * rhs))
    first_done = largest[0, 0] <= 0.0
    _, _, (sol, _, _, _) = lax.while_loop(go_on, round_of, (0, first_done, start))
    true_res = rhs - product(sol)
    good = met(sol, true_res, ACCEPT_TOL)
    to_column(sol)
    answer[...] = column[...]

    @pl.when(jnp.logical_not(good))
    def _():
        to_column(rhs)
        answer[...] = column[...]
        lanes = lax.broadcasted_iota(jnp.int32, (8, SKETCH), 1)
        below = lax.broadcasted_iota(jnp.int32, (8, LANES), 0)

        def pivot(k, carry):
            pivot_row = mat[pl.ds(k, 1), :]
            pivot_rhs = answer[pl.ds(k, 1), :]
            inverse = 1.0 / jnp.sum(jnp.where(lanes[0:1] == k, pivot_row, 0.0), axis=1, keepdims=True)

            def rows_of(group, inner):
                first = pl.multiple_of(group * 8, 8)
                here = mat[pl.ds(first, 8), :]
                factor = jnp.sum(jnp.where(lanes == k, here, 0.0), axis=1, keepdims=True) * inverse
                factor = jnp.where(below[:, 0:1] + first == k, 0.0, factor)
                mat[pl.ds(first, 8), :] = here - factor * pivot_row
                answer[pl.ds(first, 8), :] = answer[pl.ds(first, 8), :] - factor * pivot_rhs
                return inner

            return lax.fori_loop(0, SKETCH // 8, rows_of, carry)

        lax.fori_loop(0, SKETCH, pivot, 0)

        def divide(group, carry):
            first = pl.multiple_of(group * 8, 8)
            here = mat[pl.ds(first, 8), :]
            row = lax.broadcasted_iota(jnp.int32, (8, SKETCH), 0) + first
            diagonal = jnp.sum(jnp.where(lanes == row, here, 0.0), axis=1, keepdims=True)
            answer[pl.ds(first, 8), :] = answer[pl.ds(first, 8), :] / diagonal
            return carry

        lax.fori_loop(0, SKETCH // 8, divide, 0)

    for lane in range(4):
        values = jnp.sum(answer[...] * cols_ref[lane], axis=0, keepdims=True)
        out_ref[:, lane * LANES : (lane + 1) * LANES] = values * (unit * (1.0 / math.sqrt(PARAMS)))


def solve(tri, rhs, cols):
    return pl.pallas_call(
        solve_kernel,
        out_shape=(
            jax.ShapeDtypeStruct((1, DEV_COLS), jnp.float32),
            jax.ShapeDtypeStruct((OWN_ROWS, DEV_COLS), jnp.float32),
        ),
        in_specs=[pl.BlockSpec(memory_space=pltpu.VMEM)] * 3,
        out_specs=[pl.BlockSpec(memory_space=pltpu.VMEM)] * 2,
        scratch_shapes=[
            pltpu.VMEM((SKETCH, SKETCH), jnp.float32),
            pltpu.VMEM((SKETCH, LANES), jnp.float32),
            pltpu.VMEM((SKETCH, LANES), jnp.float32),
        ],
        compiler_params=pltpu.CompilerParams(vmem_limit_bytes=16 * 1024 * 1024),
        name="solve",
    )(tri, rhs, cols)


def on_device(jacobian, residual, bucket, sign_bit):
    scaling = math.sqrt(SKETCH / (DEV_ROWS * 64))
    tile = (GROUPS, LANES)
    signs = (2 * sign_bit - 1).astype(jnp.float32)
    coded = (bucket.astype(jnp.float32) + 1.0) * signs
    tri, rhs, cols = gather(jacobian, coded.reshape(tile), (residual * signs).reshape(tile), scaling)
    update, rows = solve(tri, rhs, cols)
    return (update.reshape(DEV_COLS), rows)


def solution(mesh):
    return jax.shard_map(
        on_device,
        mesh=mesh,
        in_specs=(P("dp", "col"), P("dp"), P("dp"), P("dp")),
        out_specs=(P("col"), P("dp", "col")),
        check_vma=False,
    )
```

```python
import functools
import math

import jax
import jax.numpy as jnp
from jax import lax
from jax.experimental import pallas as pl
from jax.experimental.pallas import tpu as pltpu
from jax.sharding import PartitionSpec as P

PARAMS = 4096
SKETCH = 768
DEV_ROWS = 2048
DEV_COLS = 512
OWN_ROWS = 12
LANES = 128
CHUNK = 48
BLOCK = 4 * CHUNK
GROUPS = DEV_ROWS // LANES
BLOCKS = SKETCH // LANES
TRI_ROWS = 2816
HALF = TRI_ROWS // 2
PART_A = 640
PART_B = HALF - PART_A
RHS_ROWS = 8
MESH = pl.DeviceIdType.MESH
HIGHEST = lax.Precision.HIGHEST
STOP_TOL = 1e-5
ACCEPT_TOL = 2e-5
FIRST_STEPS = 8
ROUND_STEPS = 2
MAX_ROUNDS = 30


def place():
    dp, col = lax.axis_index("dp"), lax.axis_index("col")
    return dict(x=dp % 4, near=(dp // 4) % 4, far=dp // 16, y=col // 2, core=col % 2)


def peer(me, axis, step):
    at = dict(me)
    size = 2 if axis == "core" else 4
    at[axis] = (me[axis] + step) % size
    return (at["far"] * 16 + at["near"] * 4 + at["x"], at["y"] * 2 + at["core"])


def along_z(me, step):
    z = (me["far"] * 4 + me["near"] + step + 16) % 16
    return (z * 4 + me["x"], me["y"] * 2 + me["core"])


def gather_kernel(
    scaling,
    jac_hbm,
    coded_ref,
    res_ref,
    tri_ref,
    rhs_ref,
    cols_ref,
    jac_ref,
    hot,
    acc,
    part,
    fold_in,
    x_in,
    x_sum,
    near_in,
    near_sum,
    far_in,
    res_x,
    res_near,
    res_far,
    lhs,
    rhs_t,
    tri,
    core_in,
    k_out,
    k_in_a,
    k_in_b,
    l_out_a,
    l_out_b,
    l_in_a,
    l_in_b,
    known_sem,
    load_sem,
    send_sem,
    recv_sem,
):
    me = place()
    x, near, far, y, core = (me[name] for name in ("x", "near", "far", "y", "core"))
    barrier = pltpu.get_barrier_semaphore()
    beside = [peer(me, axis, step) for axis, step in (("x", 1), ("x", 3), ("y", 1), ("y", 3), ("core", 1))]
    beside += [along_z(me, 1), along_z(me, -1)]
    for device in beside:
        pl.semaphore_signal(barrier, inc=1, device_id=device, device_id_type=MESH)

    def vouch(level, devices):
        for device in devices:
            pl.semaphore_signal(known_sem.at[level], inc=1, device_id=device, device_id_type=MESH)

    load = pltpu.make_async_copy(jac_hbm, jac_ref, load_sem)
    load.start()

    used = [0]
    sent = []

    def push(src, dst, axis, step):
        slot = used[0]
        used[0] += 1
        copy = pltpu.make_async_remote_copy(
            src_ref=src,
            dst_ref=dst,
            send_sem=send_sem.at[slot],
            recv_sem=recv_sem.at[slot],
            device_id=peer(me, axis, step),
            device_id_type=MESH,
        )
        copy.start()
        sent.append(copy)
        return copy

    def arrive(copies):
        for copy in copies:
            copy.wait_recv()

    def rows_at(first, count, unit=8):
        return pl.ds(pl.multiple_of(first, unit), count)

    def block_at(index):
        return rows_at(index % 4 * BLOCK, BLOCK, BLOCK)

    def half_of(rows, side):
        return rows_at(rows.start + side * (BLOCK // 2), BLOCK // 2, BLOCK // 2)

    def fill(block, carry):
        chunk = (block % 4) * 4 + block // 4
        targets = (lax.broadcasted_iota(jnp.int32, (CHUNK, LANES), 0) + chunk * CHUNK + 1).astype(jnp.float32)
        first = pl.multiple_of(block * CHUNK, CHUNK)
        total = jnp.zeros((CHUNK, LANES), jnp.float32)
        for group in range(GROUPS):
            code = coded_ref[group : group + 1, :]
            hit = jnp.abs(code) == targets
            total = total + jnp.where(hit, res_ref[group : group + 1, :], 0.0)
            signed = jnp.where(hit, jnp.where(code > 0.0, 1.0, -1.0), 0.0)
            hot[pl.ds(first, CHUNK), group * LANES : (group + 1) * LANES] = signed.astype(jnp.bfloat16)
        acc[pl.ds(first, CHUNK), :] = total
        return carry

    lax.fori_loop(0, SKETCH // CHUNK, fill, 0)
    load.wait()

    fold_copies = []
    for q in range(4):
        rows = block_at(near + 1 + q)
        terms = jnp.dot(hot[rows, :], jac_ref[...], preferred_element_type=jnp.float32)
        for lane in range(4):
            part[lane, rows, :] = terms[:, lane * LANES : (lane + 1) * LANES]
        if q == 0:
            pl.semaphore_wait(barrier, len(beside))
            vouch(0, [peer(me, "x", 3), peer(me, "y", 3), along_z(me, 1), along_z(me, -1)])
        two_away = (x + 2) % 4
        fold_copies.append(
            [
                push(part.at[two_away, half_of(rows, 0), :], fold_in.at[0, half_of(rows, 0), :], "x", 1),
                push(part.at[two_away, half_of(rows, 1), :], fold_in.at[1, half_of(rows, 1), :], "x", 3),
            ]
        )
    pl.semaphore_wait(known_sem.at[0], 4)
    vouch(1, [along_z(me, 2), along_z(me, -2)])

    res_row = lax.dot_general(
        jnp.ones((RHS_ROWS, LANES), jnp.float32),
        acc[...],
        (((1,), (1,)), ((), ())),
        precision=HIGHEST,
        preferred_element_type=jnp.float32,
    )
    res_x[x] = jnp.concatenate(
        [res_row[0:1, i * LANES : (i + 1) * LANES] for i in range(BLOCKS)]
        + [jnp.zeros((RHS_ROWS - BLOCKS, LANES), jnp.float32)],
        axis=0,
    )
    res_copies = [push(res_x.at[x], res_x.at[x], "x", s) for s in (1, 2, 3)]

    x_copies = []
    for q in range(4):
        rows = block_at(near + 1 + q)
        arrive(fold_copies[q])
        for step, side in ((1, 0), (3, 1)):
            index = (x + step) % 4
            there = half_of(rows, side)
            part[index, there, :] = part[index, there, :] + fold_in[side, there, :]
        x_copies.append(
            [push(part.at[(x + s) % 4, rows, :], x_in.at[side, rows, :], "x", s) for s, side in ((1, 0), (3, 1))]
        )
    pl.semaphore_wait(known_sem.at[1], 2)
    vouch(2, [along_z(me, 4), along_z(me, -4)])

    near_copies = []
    for q in range(4):
        rows = block_at(near + 1 + q)
        arrive(x_copies[q])
        summed = part[x, rows, :] + x_in[0, rows, :] + x_in[1, rows, :]
        if q < 3:
            x_sum[rows, :] = summed
            near_copies.append(push(x_sum.at[rows, :], near_in.at[near], "near", q + 1))
        else:
            near_in[near] = summed
        if q == 1:
            arrive(res_copies)
            res_near[near] = res_x[0] + res_x[1] + res_x[2] + res_x[3]
            res_copies = [push(res_near.at[near], res_near.at[near], "near", s) for s in (1, 2, 3)]
    arrive(near_copies)
    near_sum[...] = near_in[0] + near_in[1] + near_in[2] + near_in[3]

    pl.semaphore_wait(known_sem.at[2], 2)
    far_copies = []
    for s in (2, 1, 3):
        rows = rows_at((far + s) % 4 * CHUNK, CHUNK, CHUNK)
        far_copies.append(push(near_sum.at[rows, :], far_in.at[far], "far", s))
    far_in[far] = near_sum[rows_at(far * CHUNK, CHUNK, CHUNK), :]
    arrive(res_copies)
    res_far[far] = res_near[0] + res_near[1] + res_near[2] + res_near[3]
    res_copies = [push(res_far.at[far], res_far.at[far], "far", s) for s in (1, 2, 3)]
    arrive(far_copies)

    def chunk_of(at_near, at_far):
        rows = rows_at(at_near % 4 * BLOCK + at_far % 4 * CHUNK, CHUNK, CHUNK)
        return cols_ref.at[x, rows, :]

    own = chunk_of(near, far)
    own[...] = (far_in[0] + far_in[1] + far_in[2] + far_in[3]) * scaling

    far_copies = {s: push(own, own, "far", s) for s in (2, 1, 3)}
    near_copies = [push(own, own, "near", s) for s in (2, 1, 3)]
    arrive(res_copies)
    rhs_ref[...] = (res_far[0] + res_far[1] + res_far[2] + res_far[3]) * scaling
    for s in (1, 3, 2):
        arrive([far_copies[s]])
        chunk = chunk_of(near, far - s + 4)
        near_copies += [push(chunk, chunk, "near", t) for t in (2, 1, 3)]

    def share(step):
        block = cols_ref.at[x, block_at(near + step), :]
        cols_copies.append([push(block, block, "x", t) for t in (1, 3)])

    def share_on(step):
        arrive(cols_copies[step])
        for t, side in ((1, 0), (3, 1)):
            there = cols_ref.at[(x - t + 4) % 4, half_of(block_at(near + step), side), :]
            on_copies.append(push(there, there, "x", t))

    cols_copies = []
    on_copies = []
    share(0)
    arrive(near_copies)
    share(1)

    values = cols_ref[x]
    high = values.astype(jnp.bfloat16)
    low = (values - high.astype(jnp.float32)).astype(jnp.bfloat16)
    lhs[:, 0:LANES] = high
    lhs[:, LANES : 2 * LANES] = high
    lhs[:, 2 * LANES :] = low
    rhs_t[:, 0:LANES] = high
    rhs_t[:, LANES : 2 * LANES] = low
    rhs_t[:, 2 * LANES :] = high
    base = 0
    for i in range(BLOCKS):
        width = (i + 1) * LANES
        product = lax.dot_general(
            lhs[i * LANES : width, :],
            rhs_t[0:width, :],
            (((1,), (1,)), ((), ())),
            preferred_element_type=jnp.float32,
        )
        for j in range(i + 1):
            tri[base : base + LANES, :] = product[:, j * LANES : (j + 1) * LANES]
            base += LANES
    tri[base:, :] = jnp.zeros((TRI_ROWS - base, LANES), jnp.float32)

    share_on(0)

    half = core * HALF
    other = (1 - core) * HALF
    spans = ((0, PART_A), (PART_A, PART_B))
    core_copies = [
        push(tri.at[rows_at(other + first, count), :], core_in.at[first : first + count, :], "core", 1)
        for first, count in spans
    ]
    orders = (("x", "y", x, y, k_in_a, l_out_a, l_in_a), ("y", "x", y, x, k_in_b, l_out_b, l_in_b))

    first_copies = []
    for (first, count), copy, (axis, _, index, _, k_in, _, _) in zip(spans, core_copies, orders):
        arrive([copy])
        k_out[first : first + count, :] = tri[rows_at(half + first, count), :] + core_in[first : first + count, :]
        strip = count // 4
        first_copies.append(
            [
                push(k_out.at[rows_at(first + (index + s) % 4 * strip, strip), :], k_in.at[index], axis, s)
                for s in (2, 1, 3)
            ]
        )
        k_in[index] = k_out[rows_at(first + index * strip, strip), :]
    second_copies = []
    for (first, count), copies, (_, axis, _, index, k_in, l_out, l_in) in zip(spans, first_copies, orders):
        strip = count // 16
        arrive(copies)
        l_out[...] = k_in[0] + k_in[1] + k_in[2] + k_in[3]
        second_copies.append(
            [push(l_out.at[rows_at((index + s) % 4 * strip, strip), :], l_in.at[index], axis, s) for s in (2, 1, 3)]
        )
        l_in[index] = l_out[rows_at(index * strip, strip), :]
    share_on(1)
    share(2)
    second_back = []
    for (first, count), copies, (_, axis, outer, inner, _, _, l_in) in zip(spans, second_copies, orders):
        strip = count // 16
        arrive(copies)
        piece = tri_ref.at[rows_at(half + first + outer * (count // 4) + inner * strip, strip), :]
        piece[...] = l_in[0] + l_in[1] + l_in[2] + l_in[3]
        second_back.append([push(piece, piece, axis, s) for s in (2, 1, 3)])
    share_on(2)
    share(3)

    def quarter(first, count, index):
        return tri_ref.at[rows_at(half + first + index % 4 * (count // 4), count // 4), :]

    first_back = []
    last_copies = []
    for (first, count), copies, (axis, _, outer, _, _, _, _) in zip(spans, second_back, orders):
        arrive(copies)
        piece = quarter(first, count, outer)
        first_back.append([push(piece, piece, axis, s) for s in (2, 1, 3)])
        last_copies.append(push(piece, piece, "core", 1))
    share_on(3)
    for (first, count), copies, (_, _, outer, _, _, _, _) in zip(spans, first_back, orders):
        for s, copy in zip((2, 1, 3), copies):
            arrive([copy])
            piece = quarter(first, count, outer - s + 4)
            last_copies.append(push(piece, piece, "core", 1))
    assert used[0] == COPIES
    arrive(last_copies)
    arrive(on_copies)
    for copy in sent:
        copy.wait_send()


COPIES = 96


def gather(jacobian, coded, residual, scaling):
    f32 = jnp.float32
    shapes = [
        ((DEV_ROWS, DEV_COLS), jnp.bfloat16),
        ((SKETCH, DEV_ROWS), jnp.bfloat16),
        ((SKETCH, LANES), f32),
        ((4, SKETCH, LANES), f32),
        ((2, SKETCH, LANES), f32),
        ((2, SKETCH, LANES), f32),
        ((SKETCH, LANES), f32),
        ((4, BLOCK, LANES), f32),
        ((BLOCK, LANES), f32),
        ((4, CHUNK, LANES), f32),
        ((4, RHS_ROWS, LANES), f32),
        ((4, RHS_ROWS, LANES), f32),
        ((4, RHS_ROWS, LANES), f32),
        ((SKETCH, 3 * LANES), jnp.bfloat16),
        ((SKETCH, 3 * LANES), jnp.bfloat16),
        ((TRI_ROWS, LANES), f32),
        ((HALF, LANES), f32),
        ((HALF, LANES), f32),
        ((4, PART_A // 4, LANES), f32),
        ((4, PART_B // 4, LANES), f32),
        ((PART_A // 4, LANES), f32),
        ((PART_B // 4, LANES), f32),
        ((4, PART_A // 16, LANES), f32),
        ((4, PART_B // 16, LANES), f32),
    ]
    return pl.pallas_call(
        functools.partial(gather_kernel, scaling),
        out_shape=(
            jax.ShapeDtypeStruct((TRI_ROWS, LANES), f32),
            jax.ShapeDtypeStruct((RHS_ROWS, LANES), f32),
            jax.ShapeDtypeStruct((4, SKETCH, LANES), f32),
        ),
        in_specs=[pl.BlockSpec(memory_space=pl.ANY), pl.BlockSpec(memory_space=pltpu.VMEM), pl.BlockSpec(memory_space=pltpu.VMEM)],
        out_specs=[pl.BlockSpec(memory_space=pltpu.VMEM)] * 3,
        scratch_shapes=[pltpu.VMEM(shape, kind) for shape, kind in shapes]
        + [
            pltpu.SemaphoreType.REGULAR((3,)),
            pltpu.SemaphoreType.DMA,
            pltpu.SemaphoreType.DMA((COPIES,)),
            pltpu.SemaphoreType.DMA((COPIES,)),
        ],
        compiler_params=pltpu.CompilerParams(
            collective_id=0, has_side_effects=True, vmem_limit_bytes=50 * 1024 * 1024
        ),
        name="sketch_and_kernel",
    )(jacobian, coded, residual)


def total_of(row):
    return jnp.sum(row, axis=(0, 1), keepdims=True)


def solve_kernel(tri_ref, rhs_ref, cols_ref, out_ref, rows_ref, mat, column, answer):
    me = place()
    first = pl.multiple_of(me["near"] * BLOCK + me["far"] * CHUNK, CHUNK)
    for lane in range(4):
        chunk = cols_ref[lane, pl.ds(first, CHUNK), :]
        mine = chunk[:OWN_ROWS]
        for i in range(1, 4):
            mine = jnp.where(me["x"] == i, chunk[i * OWN_ROWS : (i + 1) * OWN_ROWS], mine)
        rows_ref[:, lane * LANES : (lane + 1) * LANES] = mine

    base = 0
    eye = (
        lax.broadcasted_iota(jnp.int32, (LANES, LANES), 0) == lax.broadcasted_iota(jnp.int32, (LANES, LANES), 1)
    ).astype(jnp.float32) * 0.5
    for i in range(BLOCKS):
        for j in range(i + 1):
            block = tri_ref[base : base + LANES, :] * (1.0 / PARAMS)
            base += LANES
            if i == j:
                block = block + eye
            mat[i * LANES : (i + 1) * LANES, j * LANES : (j + 1) * LANES] = block
            if i != j:
                mat[j * LANES : (j + 1) * LANES, i * LANES : (i + 1) * LANES] = block.T

    raw = jnp.concatenate([rhs_ref[i : i + 1, :] for i in range(BLOCKS)], axis=1)
    largest = jnp.max(jnp.abs(raw), axis=(0, 1), keepdims=True)
    unit = jnp.where(largest > 0, largest, 1.0)
    rhs = raw / unit

    def to_column(row):
        for i in range(BLOCKS):
            piece = jnp.broadcast_to(row[:, i * LANES : (i + 1) * LANES], (LANES, LANES))
            column[i * LANES : (i + 1) * LANES, :] = piece.T

    def product(row):
        to_column(row)
        sums = [jnp.zeros((8, LANES), jnp.float32) for _ in range(BLOCKS)]
        for group in range(SKETCH // 8):
            rows = slice(group * 8, group * 8 + 8)
            weight = column[rows, :]
            for i in range(BLOCKS):
                sums[i] = sums[i] + weight * mat[rows, i * LANES : (i + 1) * LANES]
        return jnp.concatenate([jnp.sum(s, axis=0, keepdims=True) for s in sums], axis=1)

    def met(sol, res, tol):
        scale = total_of(sol * (rhs - res)) - 0.5 * total_of(sol * sol)
        return (tol * tol * scale - 2.0 * total_of(res * res))[0, 0] >= 0.0

    def step(_, carry):
        sol, res, way = carry
        image = product(way)
        size = total_of(res * res)
        curve = total_of(way * image)
        cross = total_of(res * image)
        square = total_of(image * image)
        alpha = jnp.where(curve > 0, size / curve, 0.0)
        new_size = jnp.maximum(size + alpha * (alpha * square - 2.0 * cross), 0.0)
        beta = jnp.where(size > 0, new_size / size, 0.0)
        res = res - alpha * image
        return (sol + alpha * way, res, res + beta * way)

    def round_of(carry):
        count, _, state = carry
        state = lax.fori_loop(0, jnp.where(count == 0, FIRST_STEPS, ROUND_STEPS), step, state)
        return (count + 1, met(state[0], state[1], STOP_TOL), state)

    def go_on(carry):
        count, done, _ = carry
        return jnp.logical_and(count < MAX_ROUNDS, jnp.logical_not(done))

    start = (jnp.zeros_like(rhs), rhs, rhs)
    first_done = largest[0, 0] <= 0.0
    _, _, (sol, _, _) = lax.while_loop(go_on, round_of, (0, first_done, start))
    true_res = rhs - product(sol)
    good = met(sol, true_res, ACCEPT_TOL)
    to_column(sol)
    answer[...] = column[...]

    @pl.when(jnp.logical_not(good))
    def _():
        to_column(rhs)
        answer[...] = column[...]
        lanes = lax.broadcasted_iota(jnp.int32, (8, SKETCH), 1)
        below = lax.broadcasted_iota(jnp.int32, (8, LANES), 0)

        def pivot(k, carry):
            pivot_row = mat[pl.ds(k, 1), :]
            pivot_rhs = answer[pl.ds(k, 1), :]
            inverse = 1.0 / jnp.sum(jnp.where(lanes[0:1] == k, pivot_row, 0.0), axis=1, keepdims=True)

            def rows_of(group, inner):
                first = pl.multiple_of(group * 8, 8)
                here = mat[pl.ds(first, 8), :]
                factor = jnp.sum(jnp.where(lanes == k, here, 0.0), axis=1, keepdims=True) * inverse
                factor = jnp.where(below[:, 0:1] + first == k, 0.0, factor)
                mat[pl.ds(first, 8), :] = here - factor * pivot_row
                answer[pl.ds(first, 8), :] = answer[pl.ds(first, 8), :] - factor * pivot_rhs
                return inner

            return lax.fori_loop(0, SKETCH // 8, rows_of, carry)

        lax.fori_loop(0, SKETCH, pivot, 0)

        def divide(group, carry):
            first = pl.multiple_of(group * 8, 8)
            here = mat[pl.ds(first, 8), :]
            row = lax.broadcasted_iota(jnp.int32, (8, SKETCH), 0) + first
            diagonal = jnp.sum(jnp.where(lanes == row, here, 0.0), axis=1, keepdims=True)
            answer[pl.ds(first, 8), :] = answer[pl.ds(first, 8), :] / diagonal
            return carry

        lax.fori_loop(0, SKETCH // 8, divide, 0)

    for lane in range(4):
        values = jnp.sum(answer[...] * cols_ref[lane], axis=0, keepdims=True)
        out_ref[:, lane * LANES : (lane + 1) * LANES] = values * (unit * (1.0 / math.sqrt(PARAMS)))


def solve(tri, rhs, cols):
    return pl.pallas_call(
        solve_kernel,
        out_shape=(
            jax.ShapeDtypeStruct((1, DEV_COLS), jnp.float32),
            jax.ShapeDtypeStruct((OWN_ROWS, DEV_COLS), jnp.float32),
        ),
        in_specs=[pl.BlockSpec(memory_space=pltpu.VMEM)] * 3,
        out_specs=[pl.BlockSpec(memory_space=pltpu.VMEM)] * 2,
        scratch_shapes=[
            pltpu.VMEM((SKETCH, SKETCH), jnp.float32),
            pltpu.VMEM((SKETCH, LANES), jnp.float32),
            pltpu.VMEM((SKETCH, LANES), jnp.float32),
        ],
        compiler_params=pltpu.CompilerParams(vmem_limit_bytes=16 * 1024 * 1024),
        name="solve",
    )(tri, rhs, cols)


def on_device(jacobian, residual, bucket, sign_bit):
    scaling = math.sqrt(SKETCH / (DEV_ROWS * 64))
    tile = (GROUPS, LANES)
    signs = (2 * sign_bit - 1).astype(jnp.float32)
    coded = (bucket.astype(jnp.float32) + 1.0) * signs
    tri, rhs, cols = gather(jacobian, coded.reshape(tile), (residual * signs).reshape(tile), scaling)
    update, rows = solve(tri, rhs, cols)
    return (update.reshape(DEV_COLS), rows)


def solution(mesh):
    return jax.shard_map(
        on_device,
        mesh=mesh,
        in_specs=(P("dp", "col"), P("dp"), P("dp"), P("dp")),
        out_specs=(P("col"), P("dp", "col")),
        check_vma=False,
    )
```

```python
import functools
import math

import jax
import jax.numpy as jnp
from jax import lax
from jax.experimental import pallas as pl
from jax.experimental.pallas import tpu as pltpu
from jax.sharding import PartitionSpec as P

PARAMS = 4096
SKETCH = 768
DEV_ROWS = 2048
DEV_COLS = 512
OWN_ROWS = 12
LANES = 128
CHUNK = 48
BLOCK = 4 * CHUNK
GROUPS = DEV_ROWS // LANES
BLOCKS = SKETCH // LANES
TRI_ROWS = 2816
HALF = TRI_ROWS // 2
PART_A = 640
PART_B = HALF - PART_A
RHS_ROWS = 8
MESH = pl.DeviceIdType.MESH
HIGHEST = lax.Precision.HIGHEST
STOP_TOL = 1e-5
ACCEPT_TOL = 2e-5
FIRST_STEPS = 8
ROUND_STEPS = 2
MAX_ROUNDS = 30


def place():
    dp, col = lax.axis_index("dp"), lax.axis_index("col")
    return dict(x=dp % 4, near=(dp // 4) % 4, far=dp // 16, y=col // 2, core=col % 2)


def peer(me, axis, step):
    at = dict(me)
    size = 2 if axis == "core" else 4
    at[axis] = (me[axis] + step) % size
    return (at["far"] * 16 + at["near"] * 4 + at["x"], at["y"] * 2 + at["core"])


def along_z(me, step):
    z = (me["far"] * 4 + me["near"] + step + 16) % 16
    return (z * 4 + me["x"], me["y"] * 2 + me["core"])


def gather_kernel(
    scaling,
    jac_hbm,
    coded_ref,
    res_ref,
    tri_ref,
    rhs_ref,
    cols_ref,
    jac_ref,
    hot,
    acc,
    part,
    fold_in,
    x_in,
    x_sum,
    near_in,
    near_sum,
    far_in,
    res_x,
    res_near,
    res_far,
    lhs,
    rhs_t,
    tri,
    core_in,
    k_out,
    k_in_a,
    k_in_b,
    l_out_a,
    l_out_b,
    l_in_a,
    l_in_b,
    known_sem,
    load_sem,
    send_sem,
    recv_sem,
):
    me = place()
    x, near, far, y, core = (me[name] for name in ("x", "near", "far", "y", "core"))
    barrier = pltpu.get_barrier_semaphore()
    beside = [peer(me, axis, step) for axis, step in (("x", 1), ("x", 3), ("y", 1), ("y", 3), ("core", 1))]
    beside += [along_z(me, 1), along_z(me, -1)]
    for device in beside:
        pl.semaphore_signal(barrier, inc=1, device_id=device, device_id_type=MESH)

    def vouch(level, devices):
        for device in devices:
            pl.semaphore_signal(known_sem.at[level], inc=1, device_id=device, device_id_type=MESH)

    load = pltpu.make_async_copy(jac_hbm, jac_ref, load_sem)
    load.start()

    used = [0]
    sent = []

    def push(src, dst, axis, step):
        slot = used[0]
        used[0] += 1
        copy = pltpu.make_async_remote_copy(
            src_ref=src,
            dst_ref=dst,
            send_sem=send_sem.at[slot],
            recv_sem=recv_sem.at[slot],
            device_id=peer(me, axis, step),
            device_id_type=MESH,
        )
        copy.start()
        sent.append(copy)
        return copy

    def arrive(copies):
        for copy in copies:
            copy.wait_recv()

    def drain(keep):
        while len(sent) > keep:
            sent.pop(0).wait_send()

    def rows_at(first, count, unit=8):
        return pl.ds(pl.multiple_of(first, unit), count)

    def block_at(index):
        return rows_at(index % 4 * BLOCK, BLOCK, BLOCK)

    def half_of(rows, side):
        return rows_at(rows.start + side * (BLOCK // 2), BLOCK // 2, BLOCK // 2)

    acc[...] = jnp.zeros_like(acc)
    offset = (lax.broadcasted_iota(jnp.int32, (CHUNK, LANES), 0) + 1).astype(jnp.float32)
    for group in range(GROUPS):
        code = coded_ref[group : group + 1, :]
        target = jnp.abs(code) - offset
        signs = jnp.broadcast_to(jnp.where(code > 0.0, 1.0, -1.0), (CHUNK, LANES))
        terms = jnp.broadcast_to(res_ref[group : group + 1, :], (CHUNK, LANES))
        for block in range(SKETCH // CHUNK):
            rows = slice(block * CHUNK, (block + 1) * CHUNK)
            hit = target == float(((block % 4) * 4 + block // 4) * CHUNK)
            hot[rows, group * LANES : (group + 1) * LANES] = jnp.where(hit, signs, 0.0).astype(jnp.bfloat16)
            acc[rows, :] = acc[rows, :] + jnp.where(hit, terms, 0.0)
    load.wait()

    fold_copies = []
    for q in range(4):
        rows = block_at(near + 1 + q)
        terms = jnp.dot(hot[rows, :], jac_ref[...], preferred_element_type=jnp.float32)
        for lane in range(4):
            part[lane, rows, :] = terms[:, lane * LANES : (lane + 1) * LANES]
        if q == 0:
            pl.semaphore_wait(barrier, len(beside))
            vouch(0, [peer(me, "x", 3), peer(me, "y", 3), along_z(me, 1), along_z(me, -1)])
        two_away = (x + 2) % 4
        fold_copies.append(
            [
                push(part.at[two_away, half_of(rows, 0), :], fold_in.at[0, half_of(rows, 0), :], "x", 1),
                push(part.at[two_away, half_of(rows, 1), :], fold_in.at[1, half_of(rows, 1), :], "x", 3),
            ]
        )
    pl.semaphore_wait(known_sem.at[0], 4)
    vouch(1, [along_z(me, 2), along_z(me, -2)])

    res_row = lax.dot_general(
        jnp.ones((RHS_ROWS, LANES), jnp.float32),
        acc[...],
        (((1,), (1,)), ((), ())),
        precision=HIGHEST,
        preferred_element_type=jnp.float32,
    )
    res_x[x] = jnp.concatenate(
        [res_row[0:1, i * LANES : (i + 1) * LANES] for i in range(BLOCKS)]
        + [jnp.zeros((RHS_ROWS - BLOCKS, LANES), jnp.float32)],
        axis=0,
    )
    res_copies = [push(res_x.at[x], res_x.at[x], "x", s) for s in (1, 2, 3)]

    x_copies = []
    for q in range(4):
        rows = block_at(near + 1 + q)
        arrive(fold_copies[q])
        for step, side in ((1, 0), (3, 1)):
            index = (x + step) % 4
            there = half_of(rows, side)
            part[index, there, :] = part[index, there, :] + fold_in[side, there, :]
        x_copies.append(
            [push(part.at[(x + s) % 4, rows, :], x_in.at[side, rows, :], "x", s) for s, side in ((1, 0), (3, 1))]
        )
    pl.semaphore_wait(known_sem.at[1], 2)
    vouch(2, [along_z(me, 4), along_z(me, -4)])

    near_copies = []
    for q in range(4):
        rows = block_at(near + 1 + q)
        arrive(x_copies[q])
        summed = part[x, rows, :] + x_in[0, rows, :] + x_in[1, rows, :]
        if q < 3:
            x_sum[rows, :] = summed
            near_copies.append(push(x_sum.at[rows, :], near_in.at[near], "near", q + 1))
        else:
            near_in[near] = summed
        if q == 1:
            arrive(res_copies)
            res_near[near] = res_x[0] + res_x[1] + res_x[2] + res_x[3]
            res_copies = [push(res_near.at[near], res_near.at[near], "near", s) for s in (1, 2, 3)]
    arrive(near_copies)
    near_sum[...] = near_in[0] + near_in[1] + near_in[2] + near_in[3]

    pl.semaphore_wait(known_sem.at[2], 2)
    far_copies = []
    for s in (2, 1, 3):
        rows = rows_at((far + s) % 4 * CHUNK, CHUNK, CHUNK)
        far_copies.append(push(near_sum.at[rows, :], far_in.at[far], "far", s))
    far_in[far] = near_sum[rows_at(far * CHUNK, CHUNK, CHUNK), :]
    drain(6)
    arrive(res_copies)
    res_far[far] = res_near[0] + res_near[1] + res_near[2] + res_near[3]
    res_copies = [push(res_far.at[far], res_far.at[far], "far", s) for s in (1, 2, 3)]
    arrive(far_copies)

    def chunk_of(at_near, at_far):
        rows = rows_at(at_near % 4 * BLOCK + at_far % 4 * CHUNK, CHUNK, CHUNK)
        return cols_ref.at[x, rows, :]

    own = chunk_of(near, far)
    own[...] = (far_in[0] + far_in[1] + far_in[2] + far_in[3]) * scaling

    far_copies = {s: push(own, own, "far", s) for s in (2, 1, 3)}
    near_copies = [push(own, own, "near", s) for s in (2, 1, 3)]
    arrive(res_copies)
    rhs_ref[...] = (res_far[0] + res_far[1] + res_far[2] + res_far[3]) * scaling
    for s in (1, 3, 2):
        arrive([far_copies[s]])
        chunk = chunk_of(near, far - s + 4)
        near_copies += [push(chunk, chunk, "near", t) for t in (2, 1, 3)]

    def share(step):
        block = cols_ref.at[x, block_at(near + step), :]
        cols_copies.append([push(block, block, "x", t) for t in (1, 3)])

    def share_on(step):
        arrive(cols_copies[step])
        for t, side in ((1, 0), (3, 1)):
            there = cols_ref.at[(x - t + 4) % 4, half_of(block_at(near + step), side), :]
            on_copies.append(push(there, there, "x", t))

    cols_copies = []
    on_copies = []
    share(0)
    drain(14)
    arrive(near_copies)
    share(1)

    values = cols_ref[x]
    high = values.astype(jnp.bfloat16)
    low = (values - high.astype(jnp.float32)).astype(jnp.bfloat16)
    lhs[:, 0:LANES] = high
    lhs[:, LANES : 2 * LANES] = high
    lhs[:, 2 * LANES :] = low
    rhs_t[:, 0:LANES] = high
    rhs_t[:, LANES : 2 * LANES] = low
    rhs_t[:, 2 * LANES :] = high
    for pair in range(BLOCKS // 2):
        first, width = pair * 2 * LANES, (pair + 1) * 2 * LANES
        product = lax.dot_general(
            lhs[first:width, :],
            rhs_t[0:width, :],
            (((1,), (1,)), ((), ())),
            preferred_element_type=jnp.float32,
        )
        for i in (2 * pair, 2 * pair + 1):
            for j in range(i + 1):
                base = (i * (i + 1) // 2 + j) * LANES
                tri[base : base + LANES, :] = product[
                    i * LANES - first : (i + 1) * LANES - first, j * LANES : (j + 1) * LANES
                ]
    base = BLOCKS * (BLOCKS + 1) // 2 * LANES
    tri[base:, :] = jnp.zeros((TRI_ROWS - base, LANES), jnp.float32)

    half = core * HALF
    other = (1 - core) * HALF
    spans = ((0, PART_A), (PART_A, PART_B))
    core_copies = [
        push(tri.at[rows_at(other + first, count), :], core_in.at[first : first + count, :], "core", 1)
        for first, count in spans
    ]
    share_on(0)
    orders = (("x", "y", x, y, k_in_a, l_out_a, l_in_a), ("y", "x", y, x, k_in_b, l_out_b, l_in_b))

    first_copies = []
    for (first, count), copy, (axis, _, index, _, k_in, _, _) in zip(spans, core_copies, orders):
        arrive([copy])
        k_out[first : first + count, :] = tri[rows_at(half + first, count), :] + core_in[first : first + count, :]
        strip = count // 4
        first_copies.append(
            [
                push(k_out.at[rows_at(first + (index + s) % 4 * strip, strip), :], k_in.at[index], axis, s)
                for s in (2, 1, 3)
            ]
        )
        k_in[index] = k_out[rows_at(first + index * strip, strip), :]
    second_copies = []
    for (first, count), copies, (_, axis, _, index, k_in, l_out, l_in) in zip(spans, first_copies, orders):
        strip = count // 16
        arrive(copies)
        l_out[...] = k_in[0] + k_in[1] + k_in[2] + k_in[3]
        second_copies.append(
            [push(l_out.at[rows_at((index + s) % 4 * strip, strip), :], l_in.at[index], axis, s) for s in (2, 1, 3)]
        )
        l_in[index] = l_out[rows_at(index * strip, strip), :]
    share_on(1)
    share(2)
    drain(12)
    second_back = []
    for (first, count), copies, (_, axis, outer, inner, _, _, l_in) in zip(spans, second_copies, orders):
        strip = count // 16
        arrive(copies)
        piece = tri_ref.at[rows_at(half + first + outer * (count // 4) + inner * strip, strip), :]
        piece[...] = l_in[0] + l_in[1] + l_in[2] + l_in[3]
        second_back.append([push(piece, piece, axis, s) for s in (2, 1, 3)])
    share_on(2)
    share(3)

    def quarter(first, count, index):
        return tri_ref.at[rows_at(half + first + index % 4 * (count // 4), count // 4), :]

    first_back = []
    last_copies = []
    for (first, count), copies, (axis, _, outer, _, _, _, _) in zip(spans, second_back, orders):
        arrive(copies)
        piece = quarter(first, count, outer)
        first_back.append([push(piece, piece, axis, s) for s in (2, 1, 3)])
        last_copies.append(push(piece, piece, "core", 1))
    share_on(3)
    drain(18)
    for (first, count), copies, (_, _, outer, _, _, _, _) in zip(spans, first_back, orders):
        for s, copy in zip((2, 1, 3), copies):
            arrive([copy])
            piece = quarter(first, count, outer - s + 4)
            last_copies.append(push(piece, piece, "core", 1))
    assert used[0] == COPIES
    arrive(last_copies)
    arrive(on_copies)
    drain(0)


COPIES = 96


def gather(jacobian, coded, residual, scaling):
    f32 = jnp.float32
    shapes = [
        ((DEV_ROWS, DEV_COLS), jnp.bfloat16),
        ((SKETCH, DEV_ROWS), jnp.bfloat16),
        ((SKETCH, LANES), f32),
        ((4, SKETCH, LANES), f32),
        ((2, SKETCH, LANES), f32),
        ((2, SKETCH, LANES), f32),
        ((SKETCH, LANES), f32),
        ((4, BLOCK, LANES), f32),
        ((BLOCK, LANES), f32),
        ((4, CHUNK, LANES), f32),
        ((4, RHS_ROWS, LANES), f32),
        ((4, RHS_ROWS, LANES), f32),
        ((4, RHS_ROWS, LANES), f32),
        ((SKETCH, 3 * LANES), jnp.bfloat16),
        ((SKETCH, 3 * LANES), jnp.bfloat16),
        ((TRI_ROWS, LANES), f32),
        ((HALF, LANES), f32),
        ((HALF, LANES), f32),
        ((4, PART_A // 4, LANES), f32),
        ((4, PART_B // 4, LANES), f32),
        ((PART_A // 4, LANES), f32),
        ((PART_B // 4, LANES), f32),
        ((4, PART_A // 16, LANES), f32),
        ((4, PART_B // 16, LANES), f32),
    ]
    return pl.pallas_call(
        functools.partial(gather_kernel, scaling),
        out_shape=(
            jax.ShapeDtypeStruct((TRI_ROWS, LANES), f32),
            jax.ShapeDtypeStruct((RHS_ROWS, LANES), f32),
            jax.ShapeDtypeStruct((4, SKETCH, LANES), f32),
        ),
        in_specs=[pl.BlockSpec(memory_space=pl.ANY), pl.BlockSpec(memory_space=pltpu.VMEM), pl.BlockSpec(memory_space=pltpu.VMEM)],
        out_specs=[pl.BlockSpec(memory_space=pltpu.VMEM)] * 3,
        scratch_shapes=[pltpu.VMEM(shape, kind) for shape, kind in shapes]
        + [
            pltpu.SemaphoreType.REGULAR((3,)),
            pltpu.SemaphoreType.DMA,
            pltpu.SemaphoreType.DMA((COPIES,)),
            pltpu.SemaphoreType.DMA((COPIES,)),
        ],
        compiler_params=pltpu.CompilerParams(
            collective_id=0, has_side_effects=True, vmem_limit_bytes=50 * 1024 * 1024
        ),
        name="sketch_and_kernel",
    )(jacobian, coded, residual)


def total_of(row):
    return jnp.sum(row, axis=(0, 1), keepdims=True)


def solve_kernel(tri_ref, rhs_ref, cols_ref, out_ref, rows_ref, mat, column, answer):
    me = place()
    first = pl.multiple_of(me["near"] * BLOCK + me["far"] * CHUNK, CHUNK)
    for lane in range(4):
        chunk = cols_ref[lane, pl.ds(first, CHUNK), :]
        mine = chunk[:OWN_ROWS]
        for i in range(1, 4):
            mine = jnp.where(me["x"] == i, chunk[i * OWN_ROWS : (i + 1) * OWN_ROWS], mine)
        rows_ref[:, lane * LANES : (lane + 1) * LANES] = mine

    base = 0
    eye = (
        lax.broadcasted_iota(jnp.int32, (LANES, LANES), 0) == lax.broadcasted_iota(jnp.int32, (LANES, LANES), 1)
    ).astype(jnp.float32) * 0.5
    for i in range(BLOCKS):
        for j in range(i + 1):
            block = tri_ref[base : base + LANES, :] * (1.0 / PARAMS)
            base += LANES
            if i == j:
                block = block + eye
            mat[i * LANES : (i + 1) * LANES, j * LANES : (j + 1) * LANES] = block
            if i != j:
                mat[j * LANES : (j + 1) * LANES, i * LANES : (i + 1) * LANES] = block.T

    raw = jnp.concatenate([rhs_ref[i : i + 1, :] for i in range(BLOCKS)], axis=1)
    largest = jnp.max(jnp.abs(raw), axis=(0, 1), keepdims=True)
    unit = jnp.where(largest > 0, largest, 1.0)
    rhs = raw / unit

    def to_column(row):
        for i in range(BLOCKS):
            piece = jnp.broadcast_to(row[:, i * LANES : (i + 1) * LANES], (LANES, LANES))
            column[i * LANES : (i + 1) * LANES, :] = piece.T

    def product(row):
        to_column(row)
        sums = [jnp.zeros((8, LANES), jnp.float32) for _ in range(BLOCKS)]
        for group in range(SKETCH // 8):
            rows = slice(group * 8, group * 8 + 8)
            weight = column[rows, :]
            for i in range(BLOCKS):
                sums[i] = sums[i] + weight * mat[rows, i * LANES : (i + 1) * LANES]
        return jnp.concatenate([jnp.sum(s, axis=0, keepdims=True) for s in sums], axis=1)

    def met(sol, res, tol):
        scale = total_of(sol * (rhs - res)) - 0.5 * total_of(sol * sol)
        return (tol * tol * scale - 2.0 * total_of(res * res))[0, 0] >= 0.0

    def step(_, carry):
        sol, res, way = carry
        image = product(way)
        size = total_of(res * res)
        curve = total_of(way * image)
        cross = total_of(res * image)
        square = total_of(image * image)
        alpha = jnp.where(curve > 0, size / curve, 0.0)
        new_size = jnp.maximum(size + alpha * (alpha * square - 2.0 * cross), 0.0)
        beta = jnp.where(size > 0, new_size / size, 0.0)
        res = res - alpha * image
        return (sol + alpha * way, res, res + beta * way)

    def round_of(carry):
        count, _, state = carry
        state = lax.fori_loop(0, jnp.where(count == 0, FIRST_STEPS, ROUND_STEPS), step, state)
        return (count + 1, met(state[0], state[1], STOP_TOL), state)

    def go_on(carry):
        count, done, _ = carry
        return jnp.logical_and(count < MAX_ROUNDS, jnp.logical_not(done))

    start = (jnp.zeros_like(rhs), rhs, rhs)
    first_done = largest[0, 0] <= 0.0
    _, _, (sol, _, _) = lax.while_loop(go_on, round_of, (0, first_done, start))
    true_res = rhs - product(sol)
    good = met(sol, true_res, ACCEPT_TOL)
    to_column(sol)
    answer[...] = column[...]

    @pl.when(jnp.logical_not(good))
    def _():
        to_column(rhs)
        answer[...] = column[...]
        lanes = lax.broadcasted_iota(jnp.int32, (8, SKETCH), 1)
        below = lax.broadcasted_iota(jnp.int32, (8, LANES), 0)

        def pivot(k, carry):
            pivot_row = mat[pl.ds(k, 1), :]
            pivot_rhs = answer[pl.ds(k, 1), :]
            inverse = 1.0 / jnp.sum(jnp.where(lanes[0:1] == k, pivot_row, 0.0), axis=1, keepdims=True)

            def rows_of(group, inner):
                first = pl.multiple_of(group * 8, 8)
                here = mat[pl.ds(first, 8), :]
                factor = jnp.sum(jnp.where(lanes == k, here, 0.0), axis=1, keepdims=True) * inverse
                factor = jnp.where(below[:, 0:1] + first == k, 0.0, factor)
                mat[pl.ds(first, 8), :] = here - factor * pivot_row
                answer[pl.ds(first, 8), :] = answer[pl.ds(first, 8), :] - factor * pivot_rhs
                return inner

            return lax.fori_loop(0, SKETCH // 8, rows_of, carry)

        lax.fori_loop(0, SKETCH, pivot, 0)

        def divide(group, carry):
            first = pl.multiple_of(group * 8, 8)
            here = mat[pl.ds(first, 8), :]
            row = lax.broadcasted_iota(jnp.int32, (8, SKETCH), 0) + first
            diagonal = jnp.sum(jnp.where(lanes == row, here, 0.0), axis=1, keepdims=True)
            answer[pl.ds(first, 8), :] = answer[pl.ds(first, 8), :] / diagonal
            return carry

        lax.fori_loop(0, SKETCH // 8, divide, 0)

    for lane in range(4):
        values = jnp.sum(answer[...] * cols_ref[lane], axis=0, keepdims=True)
        out_ref[:, lane * LANES : (lane + 1) * LANES] = values * (unit * (1.0 / math.sqrt(PARAMS)))


def solve(tri, rhs, cols):
    return pl.pallas_call(
        solve_kernel,
        out_shape=(
            jax.ShapeDtypeStruct((1, DEV_COLS), jnp.float32),
            jax.ShapeDtypeStruct((OWN_ROWS, DEV_COLS), jnp.float32),
        ),
        in_specs=[pl.BlockSpec(memory_space=pltpu.VMEM)] * 3,
        out_specs=[pl.BlockSpec(memory_space=pltpu.VMEM)] * 2,
        scratch_shapes=[
            pltpu.VMEM((SKETCH, SKETCH), jnp.float32),
            pltpu.VMEM((SKETCH, LANES), jnp.float32),
            pltpu.VMEM((SKETCH, LANES), jnp.float32),
        ],
        compiler_params=pltpu.CompilerParams(vmem_limit_bytes=16 * 1024 * 1024),
        name="solve",
    )(tri, rhs, cols)


def on_device(jacobian, residual, bucket, sign_bit):
    scaling = math.sqrt(SKETCH / (DEV_ROWS * 64))
    tile = (GROUPS, LANES)
    signs = (2 * sign_bit - 1).astype(jnp.float32)
    coded = (bucket.astype(jnp.float32) + 1.0) * signs
    tri, rhs, cols = gather(jacobian, coded.reshape(tile), (residual * signs).reshape(tile), scaling)
    update, rows = solve(tri, rhs, cols)
    return (update.reshape(DEV_COLS), rows)


def solution(mesh):
    return jax.shard_map(
        on_device,
        mesh=mesh,
        in_specs=(P("dp", "col"), P("dp"), P("dp"), P("dp")),
        out_specs=(P("col"), P("dp", "col")),
        check_vma=False,
    )
```

```python
import functools
import math

import jax
import jax.numpy as jnp
from jax import lax
from jax.experimental import pallas as pl
from jax.experimental.pallas import tpu as pltpu
from jax.sharding import PartitionSpec as P

PARAMS = 4096
SKETCH = 768
DEV_ROWS = 2048
DEV_COLS = 512
OWN_ROWS = 12
LANES = 128
CHUNK = 48
BLOCK = 4 * CHUNK
GROUPS = DEV_ROWS // LANES
BLOCKS = SKETCH // LANES
TRI_ROWS = 2816
HALF = TRI_ROWS // 2
PART_A = 640
PART_B = HALF - PART_A
RHS_ROWS = 8
MESH = pl.DeviceIdType.MESH
HIGHEST = lax.Precision.HIGHEST
STOP_TOL = 1e-5
ACCEPT_TOL = 2e-5
FIRST_STEPS = 10
ROUND_STEPS = 2
MAX_ROUNDS = 30


def place():
    dp, col = lax.axis_index("dp"), lax.axis_index("col")
    return dict(x=dp % 4, near=(dp // 4) % 4, far=dp // 16, y=col // 2, core=col % 2)


def peer(me, axis, step):
    at = dict(me)
    size = 2 if axis == "core" else 4
    at[axis] = (me[axis] + step) % size
    return (at["far"] * 16 + at["near"] * 4 + at["x"], at["y"] * 2 + at["core"])


def along_z(me, step):
    z = (me["far"] * 4 + me["near"] + step + 16) % 16
    return (z * 4 + me["x"], me["y"] * 2 + me["core"])


def gather_kernel(
    scaling,
    jac_hbm,
    coded_ref,
    res_ref,
    tri_ref,
    rhs_ref,
    cols_ref,
    jac_ref,
    hot,
    acc,
    part,
    fold_in,
    x_in,
    x_sum,
    near_in,
    near_sum,
    far_in,
    res_x,
    res_near,
    res_far,
    lhs,
    rhs_t,
    tri,
    core_in,
    k_out,
    k_in_a,
    k_in_b,
    l_out_a,
    l_out_b,
    l_in_a,
    l_in_b,
    known_sem,
    load_sem,
    send_sem,
    recv_sem,
):
    me = place()
    x, near, far, y, core = (me[name] for name in ("x", "near", "far", "y", "core"))
    barrier = pltpu.get_barrier_semaphore()
    beside = [peer(me, axis, step) for axis, step in (("x", 1), ("x", 3), ("y", 1), ("y", 3), ("core", 1))]
    beside += [along_z(me, 1), along_z(me, -1)]
    for device in beside:
        pl.semaphore_signal(barrier, inc=1, device_id=device, device_id_type=MESH)

    def vouch(level, devices):
        for device in devices:
            pl.semaphore_signal(known_sem.at[level], inc=1, device_id=device, device_id_type=MESH)

    load = pltpu.make_async_copy(jac_hbm, jac_ref, load_sem)
    load.start()

    used = [0]
    sent = []

    def push(src, dst, axis, step):
        slot = used[0]
        used[0] += 1
        copy = pltpu.make_async_remote_copy(
            src_ref=src,
            dst_ref=dst,
            send_sem=send_sem.at[slot],
            recv_sem=recv_sem.at[slot],
            device_id=peer(me, axis, step),
            device_id_type=MESH,
        )
        copy.start()
        sent.append(copy)
        return copy

    def arrive(copies):
        for copy in copies:
            copy.wait_recv()

    def drain(keep):
        while len(sent) > keep:
            sent.pop(0).wait_send()

    def rows_at(first, count, unit=8):
        return pl.ds(pl.multiple_of(first, unit), count)

    def block_at(index):
        return rows_at(index % 4 * BLOCK, BLOCK, BLOCK)

    def half_of(rows, side):
        return rows_at(rows.start + side * (BLOCK // 2), BLOCK // 2, BLOCK // 2)

    acc[...] = jnp.zeros_like(acc)
    offset = (lax.broadcasted_iota(jnp.int32, (CHUNK, LANES), 0) + 1).astype(jnp.float32)
    for group in range(GROUPS):
        code = coded_ref[group : group + 1, :]
        target = jnp.abs(code) - offset
        signs = jnp.broadcast_to(jnp.where(code > 0.0, 1.0, -1.0), (CHUNK, LANES))
        terms = jnp.broadcast_to(res_ref[group : group + 1, :], (CHUNK, LANES))
        for block in range(SKETCH // CHUNK):
            rows = slice(block * CHUNK, (block + 1) * CHUNK)
            hit = target == float(((block % 4) * 4 + block // 4) * CHUNK)
            hot[rows, group * LANES : (group + 1) * LANES] = jnp.where(hit, signs, 0.0).astype(jnp.bfloat16)
            acc[rows, :] = acc[rows, :] + jnp.where(hit, terms, 0.0)
    load.wait()

    fold_copies = []
    for q in range(4):
        rows = block_at(near + 1 + q)
        terms = jnp.dot(hot[rows, :], jac_ref[...], preferred_element_type=jnp.float32)
        for lane in range(4):
            part[lane, rows, :] = terms[:, lane * LANES : (lane + 1) * LANES]
        if q == 0:
            pl.semaphore_wait(barrier, len(beside))
            vouch(0, [peer(me, "x", 3), peer(me, "y", 3), along_z(me, 1), along_z(me, -1)])
        two_away = (x + 2) % 4
        fold_copies.append(
            [
                push(part.at[two_away, half_of(rows, 0), :], fold_in.at[0, half_of(rows, 0), :], "x", 1),
                push(part.at[two_away, half_of(rows, 1), :], fold_in.at[1, half_of(rows, 1), :], "x", 3),
            ]
        )
    pl.semaphore_wait(known_sem.at[0], 4)
    vouch(1, [along_z(me, 2), along_z(me, -2)])

    res_row = lax.dot_general(
        jnp.ones((RHS_ROWS, LANES), jnp.float32),
        acc[...],
        (((1,), (1,)), ((), ())),
        precision=HIGHEST,
        preferred_element_type=jnp.float32,
    )
    res_x[x] = jnp.concatenate(
        [res_row[0:1, i * LANES : (i + 1) * LANES] for i in range(BLOCKS)]
        + [jnp.zeros((RHS_ROWS - BLOCKS, LANES), jnp.float32)],
        axis=0,
    )
    res_copies = [push(res_x.at[x], res_x.at[x], "x", s) for s in (1, 2, 3)]

    x_copies = []
    for q in range(4):
        rows = block_at(near + 1 + q)
        arrive(fold_copies[q])
        for step, side in ((1, 0), (3, 1)):
            index = (x + step) % 4
            there = half_of(rows, side)
            part[index, there, :] = part[index, there, :] + fold_in[side, there, :]
        x_copies.append(
            [push(part.at[(x + s) % 4, rows, :], x_in.at[side, rows, :], "x", s) for s, side in ((1, 0), (3, 1))]
        )
    pl.semaphore_wait(known_sem.at[1], 2)
    vouch(2, [along_z(me, 4), along_z(me, -4)])

    near_copies = []
    for q in range(4):
        rows = block_at(near + 1 + q)
        arrive(x_copies[q])
        summed = part[x, rows, :] + x_in[0, rows, :] + x_in[1, rows, :]
        if q < 3:
            x_sum[rows, :] = summed
            near_copies.append(push(x_sum.at[rows, :], near_in.at[near], "near", q + 1))
        else:
            near_in[near] = summed
        if q == 1:
            arrive(res_copies)
            res_near[near] = res_x[0] + res_x[1] + res_x[2] + res_x[3]
            res_copies = [push(res_near.at[near], res_near.at[near], "near", s) for s in (1, 2, 3)]
    arrive(near_copies)
    near_sum[...] = near_in[0] + near_in[1] + near_in[2] + near_in[3]

    pl.semaphore_wait(known_sem.at[2], 2)
    far_copies = []
    for s in (2, 1, 3):
        rows = rows_at((far + s) % 4 * CHUNK, CHUNK, CHUNK)
        far_copies.append(push(near_sum.at[rows, :], far_in.at[far], "far", s))
    far_in[far] = near_sum[rows_at(far * CHUNK, CHUNK, CHUNK), :]
    drain(6)
    arrive(res_copies)
    res_far[far] = res_near[0] + res_near[1] + res_near[2] + res_near[3]
    res_copies = [push(res_far.at[far], res_far.at[far], "far", s) for s in (1, 2, 3)]
    arrive(far_copies)

    def chunk_of(at_near, at_far):
        rows = rows_at(at_near % 4 * BLOCK + at_far % 4 * CHUNK, CHUNK, CHUNK)
        return cols_ref.at[x, rows, :]

    own = chunk_of(near, far)
    own[...] = (far_in[0] + far_in[1] + far_in[2] + far_in[3]) * scaling

    far_copies = {s: push(own, own, "far", s) for s in (2, 1, 3)}
    near_copies = [push(own, own, "near", s) for s in (2, 1, 3)]
    arrive(res_copies)
    rhs_ref[...] = (res_far[0] + res_far[1] + res_far[2] + res_far[3]) * scaling
    for s in (1, 3, 2):
        arrive([far_copies[s]])
        chunk = chunk_of(near, far - s + 4)
        near_copies += [push(chunk, chunk, "near", t) for t in (2, 1, 3)]

    def share(step):
        block = cols_ref.at[x, block_at(near + step), :]
        cols_copies.append([push(block, block, "x", t) for t in (1, 3)])

    def share_on(step):
        arrive(cols_copies[step])
        for t, side in ((1, 0), (3, 1)):
            there = cols_ref.at[(x - t + 4) % 4, half_of(block_at(near + step), side), :]
            on_copies.append(push(there, there, "x", t))

    cols_copies = []
    on_copies = []
    share(0)
    drain(14)
    arrive(near_copies)
    share(1)

    values = cols_ref[x]
    high = values.astype(jnp.bfloat16)
    low = (values - high.astype(jnp.float32)).astype(jnp.bfloat16)
    lhs[:, 0:LANES] = high
    lhs[:, LANES : 2 * LANES] = high
    lhs[:, 2 * LANES :] = low
    rhs_t[:, 0:LANES] = high
    rhs_t[:, LANES : 2 * LANES] = low
    rhs_t[:, 2 * LANES :] = high
    for pair in range(BLOCKS // 2):
        first, width = pair * 2 * LANES, (pair + 1) * 2 * LANES
        product = lax.dot_general(
            lhs[first:width, :],
            rhs_t[0:width, :],
            (((1,), (1,)), ((), ())),
            preferred_element_type=jnp.float32,
        )
        for i in (2 * pair, 2 * pair + 1):
            for j in range(i + 1):
                base = (i * (i + 1) // 2 + j) * LANES
                tri[base : base + LANES, :] = product[
                    i * LANES - first : (i + 1) * LANES - first, j * LANES : (j + 1) * LANES
                ]
    base = BLOCKS * (BLOCKS + 1) // 2 * LANES
    tri[base:, :] = jnp.zeros((TRI_ROWS - base, LANES), jnp.float32)

    half = core * HALF
    other = (1 - core) * HALF
    spans = ((0, PART_A), (PART_A, PART_B))
    core_copies = [
        push(tri.at[rows_at(other + first, count), :], core_in.at[first : first + count, :], "core", 1)
        for first, count in spans
    ]
    orders = (("x", "y", x, y, k_in_a, l_out_a, l_in_a), ("y", "x", y, x, k_in_b, l_out_b, l_in_b))

    first_copies = []
    for (first, count), copy, (axis, _, index, _, k_in, _, _) in zip(spans, core_copies, orders):
        arrive([copy])
        k_out[first : first + count, :] = tri[rows_at(half + first, count), :] + core_in[first : first + count, :]
        strip = count // 4
        first_copies.append(
            [
                push(k_out.at[rows_at(first + (index + s) % 4 * strip, strip), :], k_in.at[index], axis, s)
                for s in (2, 1, 3)
            ]
        )
        k_in[index] = k_out[rows_at(first + index * strip, strip), :]
    share_on(0)
    share(2)
    second_copies = []
    for (first, count), copies, (_, axis, _, index, k_in, l_out, l_in) in zip(spans, first_copies, orders):
        strip = count // 16
        arrive(copies)
        l_out[...] = k_in[0] + k_in[1] + k_in[2] + k_in[3]
        second_copies.append(
            [push(l_out.at[rows_at((index + s) % 4 * strip, strip), :], l_in.at[index], axis, s) for s in (2, 1, 3)]
        )
        l_in[index] = l_out[rows_at(index * strip, strip), :]
    share_on(1)
    share(3)
    drain(12)
    second_back = []
    for (first, count), copies, (_, axis, outer, inner, _, _, l_in) in zip(spans, second_copies, orders):
        strip = count // 16
        arrive(copies)
        piece = tri_ref.at[rows_at(half + first + outer * (count // 4) + inner * strip, strip), :]
        piece[...] = l_in[0] + l_in[1] + l_in[2] + l_in[3]
        second_back.append([push(piece, piece, axis, s) for s in (2, 1, 3)])
    share_on(2)

    def quarter(first, count, index):
        return tri_ref.at[rows_at(half + first + index % 4 * (count // 4), count // 4), :]

    first_back = []
    last_copies = []
    for (first, count), copies, (axis, _, outer, _, _, _, _) in zip(spans, second_back, orders):
        arrive(copies)
        piece = quarter(first, count, outer)
        first_back.append([push(piece, piece, axis, s) for s in (2, 1, 3)])
        last_copies.append(push(piece, piece, "core", 1))
    share_on(3)
    drain(18)
    for (first, count), copies, (_, _, outer, _, _, _, _) in zip(spans, first_back, orders):
        for s, copy in zip((2, 1, 3), copies):
            arrive([copy])
            piece = quarter(first, count, outer - s + 4)
            last_copies.append(push(piece, piece, "core", 1))
    assert used[0] == COPIES
    arrive(last_copies)
    arrive(on_copies)
    drain(0)


COPIES = 96


def gather(jacobian, coded, residual, scaling):
    f32 = jnp.float32
    shapes = [
        ((DEV_ROWS, DEV_COLS), jnp.bfloat16),
        ((SKETCH, DEV_ROWS), jnp.bfloat16),
        ((SKETCH, LANES), f32),
        ((4, SKETCH, LANES), f32),
        ((2, SKETCH, LANES), f32),
        ((2, SKETCH, LANES), f32),
        ((SKETCH, LANES), f32),
        ((4, BLOCK, LANES), f32),
        ((BLOCK, LANES), f32),
        ((4, CHUNK, LANES), f32),
        ((4, RHS_ROWS, LANES), f32),
        ((4, RHS_ROWS, LANES), f32),
        ((4, RHS_ROWS, LANES), f32),
        ((SKETCH, 3 * LANES), jnp.bfloat16),
        ((SKETCH, 3 * LANES), jnp.bfloat16),
        ((TRI_ROWS, LANES), f32),
        ((HALF, LANES), f32),
        ((HALF, LANES), f32),
        ((4, PART_A // 4, LANES), f32),
        ((4, PART_B // 4, LANES), f32),
        ((PART_A // 4, LANES), f32),
        ((PART_B // 4, LANES), f32),
        ((4, PART_A // 16, LANES), f32),
        ((4, PART_B // 16, LANES), f32),
    ]
    return pl.pallas_call(
        functools.partial(gather_kernel, scaling),
        out_shape=(
            jax.ShapeDtypeStruct((TRI_ROWS, LANES), f32),
            jax.ShapeDtypeStruct((RHS_ROWS, LANES), f32),
            jax.ShapeDtypeStruct((4, SKETCH, LANES), f32),
        ),
        in_specs=[pl.BlockSpec(memory_space=pl.ANY), pl.BlockSpec(memory_space=pltpu.VMEM), pl.BlockSpec(memory_space=pltpu.VMEM)],
        out_specs=[pl.BlockSpec(memory_space=pltpu.VMEM)] * 3,
        scratch_shapes=[pltpu.VMEM(shape, kind) for shape, kind in shapes]
        + [
            pltpu.SemaphoreType.REGULAR((3,)),
            pltpu.SemaphoreType.DMA,
            pltpu.SemaphoreType.DMA((COPIES,)),
            pltpu.SemaphoreType.DMA((COPIES,)),
        ],
        compiler_params=pltpu.CompilerParams(
            collective_id=0, has_side_effects=True, vmem_limit_bytes=50 * 1024 * 1024
        ),
        name="sketch_and_kernel",
    )(jacobian, coded, residual)


def total_of(row):
    return jnp.sum(row, axis=(0, 1), keepdims=True)


def solve_kernel(tri_ref, rhs_ref, cols_ref, out_ref, rows_ref, mat, column, answer):
    me = place()
    first = pl.multiple_of(me["near"] * BLOCK + me["far"] * CHUNK, CHUNK)
    for lane in range(4):
        chunk = cols_ref[lane, pl.ds(first, CHUNK), :]
        mine = chunk[:OWN_ROWS]
        for i in range(1, 4):
            mine = jnp.where(me["x"] == i, chunk[i * OWN_ROWS : (i + 1) * OWN_ROWS], mine)
        rows_ref[:, lane * LANES : (lane + 1) * LANES] = mine

    base = 0
    eye = (
        lax.broadcasted_iota(jnp.int32, (LANES, LANES), 0) == lax.broadcasted_iota(jnp.int32, (LANES, LANES), 1)
    ).astype(jnp.float32) * 0.5
    for i in range(BLOCKS):
        for j in range(i + 1):
            block = tri_ref[base : base + LANES, :] * (1.0 / PARAMS)
            base += LANES
            if i == j:
                block = block + eye
            mat[i * LANES : (i + 1) * LANES, j * LANES : (j + 1) * LANES] = block
            if i != j:
                mat[j * LANES : (j + 1) * LANES, i * LANES : (i + 1) * LANES] = block.T

    raw = jnp.concatenate([rhs_ref[i : i + 1, :] for i in range(BLOCKS)], axis=1)
    largest = jnp.max(jnp.abs(raw), axis=(0, 1), keepdims=True)
    unit = jnp.where(largest > 0, largest, 1.0)
    rhs = raw / unit

    def to_column(row):
        for i in range(BLOCKS):
            piece = jnp.broadcast_to(row[:, i * LANES : (i + 1) * LANES], (LANES, LANES))
            column[i * LANES : (i + 1) * LANES, :] = piece.T

    def product(row):
        to_column(row)
        sums = [jnp.zeros((8, LANES), jnp.float32) for _ in range(BLOCKS)]
        for group in range(SKETCH // 8):
            rows = slice(group * 8, group * 8 + 8)
            weight = column[rows, :]
            for i in range(BLOCKS):
                sums[i] = sums[i] + weight * mat[rows, i * LANES : (i + 1) * LANES]
        return jnp.concatenate([jnp.sum(s, axis=0, keepdims=True) for s in sums], axis=1)

    def met(sol, res, tol):
        scale = total_of(sol * (rhs - res)) - 0.5 * total_of(sol * sol)
        return (tol * tol * scale - 2.0 * total_of(res * res))[0, 0] >= 0.0

    def step(_, carry):
        sol, res, way = carry
        image = product(way)
        size = total_of(res * res)
        curve = total_of(way * image)
        cross = total_of(res * image)
        square = total_of(image * image)
        alpha = jnp.where(curve > 0, size / curve, 0.0)
        new_size = jnp.maximum(size + alpha * (alpha * square - 2.0 * cross), 0.0)
        beta = jnp.where(size > 0, new_size / size, 0.0)
        res = res - alpha * image
        return (sol + alpha * way, res, res + beta * way)

    def round_of(carry):
        count, _, state = carry
        state = lax.fori_loop(0, jnp.where(count == 0, FIRST_STEPS, ROUND_STEPS), step, state)
        return (count + 1, met(state[0], state[1], STOP_TOL), state)

    def go_on(carry):
        count, done, _ = carry
        return jnp.logical_and(count < MAX_ROUNDS, jnp.logical_not(done))

    start = (jnp.zeros_like(rhs), rhs, rhs)
    first_done = largest[0, 0] <= 0.0
    _, _, (sol, _, _) = lax.while_loop(go_on, round_of, (0, first_done, start))
    true_res = rhs - product(sol)
    good = met(sol, true_res, ACCEPT_TOL)
    answer[...] = column[...]

    @pl.when(jnp.logical_not(good))
    def _():
        to_column(rhs)
        answer[...] = column[...]
        lanes = lax.broadcasted_iota(jnp.int32, (8, SKETCH), 1)
        below = lax.broadcasted_iota(jnp.int32, (8, LANES), 0)

        def pivot(k, carry):
            pivot_row = mat[pl.ds(k, 1), :]
            pivot_rhs = answer[pl.ds(k, 1), :]
            inverse = 1.0 / jnp.sum(jnp.where(lanes[0:1] == k, pivot_row, 0.0), axis=1, keepdims=True)

            def rows_of(group, inner):
                first = pl.multiple_of(group * 8, 8)
                here = mat[pl.ds(first, 8), :]
                factor = jnp.sum(jnp.where(lanes == k, here, 0.0), axis=1, keepdims=True) * inverse
                factor = jnp.where(below[:, 0:1] + first == k, 0.0, factor)
                mat[pl.ds(first, 8), :] = here - factor * pivot_row
                answer[pl.ds(first, 8), :] = answer[pl.ds(first, 8), :] - factor * pivot_rhs
                return inner

            return lax.fori_loop(0, SKETCH // 8, rows_of, carry)

        lax.fori_loop(0, SKETCH, pivot, 0)

        def divide(group, carry):
            first = pl.multiple_of(group * 8, 8)
            here = mat[pl.ds(first, 8), :]
            row = lax.broadcasted_iota(jnp.int32, (8, SKETCH), 0) + first
            diagonal = jnp.sum(jnp.where(lanes == row, here, 0.0), axis=1, keepdims=True)
            answer[pl.ds(first, 8), :] = answer[pl.ds(first, 8), :] / diagonal
            return carry

        lax.fori_loop(0, SKETCH // 8, divide, 0)

    for lane in range(4):
        values = jnp.sum(answer[...] * cols_ref[lane], axis=0, keepdims=True)
        out_ref[:, lane * LANES : (lane + 1) * LANES] = values * (unit * (1.0 / math.sqrt(PARAMS)))


def solve(tri, rhs, cols):
    return pl.pallas_call(
        solve_kernel,
        out_shape=(
            jax.ShapeDtypeStruct((1, DEV_COLS), jnp.float32),
            jax.ShapeDtypeStruct((OWN_ROWS, DEV_COLS), jnp.float32),
        ),
        in_specs=[pl.BlockSpec(memory_space=pltpu.VMEM)] * 3,
        out_specs=[pl.BlockSpec(memory_space=pltpu.VMEM)] * 2,
        scratch_shapes=[
            pltpu.VMEM((SKETCH, SKETCH), jnp.float32),
            pltpu.VMEM((SKETCH, LANES), jnp.float32),
            pltpu.VMEM((SKETCH, LANES), jnp.float32),
        ],
        compiler_params=pltpu.CompilerParams(vmem_limit_bytes=16 * 1024 * 1024),
        name="solve",
    )(tri, rhs, cols)


def on_device(jacobian, residual, bucket, sign_bit):
    scaling = math.sqrt(SKETCH / (DEV_ROWS * 64))
    tile = (GROUPS, LANES)
    signs = (2 * sign_bit - 1).astype(jnp.float32)
    coded = (bucket.astype(jnp.float32) + 1.0) * signs
    tri, rhs, cols = gather(jacobian, coded.reshape(tile), (residual * signs).reshape(tile), scaling)
    update, rows = solve(tri, rhs, cols)
    return (update.reshape(DEV_COLS), rows)


def solution(mesh):
    return jax.shard_map(
        on_device,
        mesh=mesh,
        in_specs=(P("dp", "col"), P("dp"), P("dp"), P("dp")),
        out_specs=(P("col"), P("dp", "col")),
        check_vma=False,
    )
```

```python
import functools
import math

import jax
import jax.numpy as jnp
from jax import lax
from jax.experimental import pallas as pl
from jax.experimental.pallas import tpu as pltpu
from jax.sharding import PartitionSpec as P

PARAMS = 4096
SKETCH = 768
DEV_ROWS = 2048
DEV_COLS = 512
OWN_ROWS = 12
LANES = 128
CHUNK = 48
BLOCK = 4 * CHUNK
GROUPS = DEV_ROWS // LANES
BLOCKS = SKETCH // LANES
TRI_ROWS = 2816
HALF = TRI_ROWS // 2
PART_A = 640
PART_B = HALF - PART_A
RHS_ROWS = 8
MESH = pl.DeviceIdType.MESH
HIGHEST = lax.Precision.HIGHEST
STOP_TOL = 1e-5
ACCEPT_TOL = 2e-5
FIRST_STEPS = 10
ROUND_STEPS = 2
MAX_ROUNDS = 30


def place():
    dp, col = lax.axis_index("dp"), lax.axis_index("col")
    return dict(x=dp % 4, near=(dp // 4) % 4, far=dp // 16, y=col // 2, core=col % 2)


def peer(me, axis, step):
    at = dict(me)
    size = 2 if axis == "core" else 4
    at[axis] = (me[axis] + step) % size
    return (at["far"] * 16 + at["near"] * 4 + at["x"], at["y"] * 2 + at["core"])


def along_z(me, step):
    z = (me["far"] * 4 + me["near"] + step + 16) % 16
    return (z * 4 + me["x"], me["y"] * 2 + me["core"])


def gather_kernel(
    scaling,
    jac_hbm,
    coded_ref,
    res_ref,
    tri_ref,
    rhs_ref,
    cols_ref,
    jac_ref,
    hot,
    acc,
    part,
    fold_in,
    x_in,
    x_sum,
    near_in,
    near_sum,
    far_in,
    res_x,
    res_near,
    res_far,
    lhs,
    rhs_t,
    tri,
    core_in,
    k_out,
    k_in_a,
    k_in_b,
    l_out_a,
    l_out_b,
    l_in_a,
    l_in_b,
    known_sem,
    load_sem,
    send_sem,
    recv_sem,
):
    me = place()
    x, near, far, y, core = (me[name] for name in ("x", "near", "far", "y", "core"))
    barrier = pltpu.get_barrier_semaphore()
    beside = [peer(me, axis, step) for axis, step in (("x", 1), ("x", 3), ("y", 1), ("y", 3), ("core", 1))]
    beside += [along_z(me, 1), along_z(me, -1)]
    for device in beside:
        pl.semaphore_signal(barrier, inc=1, device_id=device, device_id_type=MESH)

    def vouch(level, devices):
        for device in devices:
            pl.semaphore_signal(known_sem.at[level], inc=1, device_id=device, device_id_type=MESH)

    load = pltpu.make_async_copy(jac_hbm, jac_ref, load_sem)
    load.start()

    used = [0]
    sent = []

    def push(src, dst, axis, step):
        slot = used[0]
        used[0] += 1
        copy = pltpu.make_async_remote_copy(
            src_ref=src,
            dst_ref=dst,
            send_sem=send_sem.at[slot],
            recv_sem=recv_sem.at[slot],
            device_id=peer(me, axis, step),
            device_id_type=MESH,
        )
        copy.start()
        sent.append(copy)
        return copy

    def arrive(copies):
        for copy in copies:
            copy.wait_recv()

    def drain(keep):
        while len(sent) > keep:
            sent.pop(0).wait_send()

    def rows_at(first, count, unit=8):
        return pl.ds(pl.multiple_of(first, unit), count)

    def block_at(index):
        return rows_at(index % 4 * BLOCK, BLOCK, BLOCK)

    def half_of(rows, side):
        return rows_at(rows.start + side * (BLOCK // 2), BLOCK // 2, BLOCK // 2)

    acc[...] = jnp.zeros_like(acc)
    offset = (lax.broadcasted_iota(jnp.int32, (CHUNK, LANES), 0) + 1).astype(jnp.float32)
    for group in range(GROUPS):
        code = coded_ref[group : group + 1, :]
        target = jnp.abs(code) - offset
        signs = jnp.broadcast_to(jnp.where(code > 0.0, 1.0, -1.0), (CHUNK, LANES))
        terms = jnp.broadcast_to(res_ref[group : group + 1, :], (CHUNK, LANES))
        for block in range(SKETCH // CHUNK):
            rows = slice(block * CHUNK, (block + 1) * CHUNK)
            hit = target == float(((block % 4) * 4 + block // 4) * CHUNK)
            hot[rows, group * LANES : (group + 1) * LANES] = jnp.where(hit, signs, 0.0).astype(jnp.bfloat16)
            acc[rows, :] = acc[rows, :] + jnp.where(hit, terms, 0.0)
    load.wait()

    fold_copies = []
    for q in range(4):
        rows = block_at(near + 1 + q)
        terms = jnp.dot(hot[rows, :], jac_ref[...], preferred_element_type=jnp.float32)
        for lane in range(4):
            part[lane, rows, :] = terms[:, lane * LANES : (lane + 1) * LANES]
        if q == 0:
            pl.semaphore_wait(barrier, len(beside))
            vouch(0, [peer(me, "x", 3), peer(me, "y", 3), along_z(me, 1), along_z(me, -1)])
        two_away = (x + 2) % 4
        fold_copies.append(
            [
                push(part.at[two_away, half_of(rows, 0), :], fold_in.at[0, half_of(rows, 0), :], "x", 1),
                push(part.at[two_away, half_of(rows, 1), :], fold_in.at[1, half_of(rows, 1), :], "x", 3),
            ]
        )
    pl.semaphore_wait(known_sem.at[0], 4)
    vouch(1, [along_z(me, 2), along_z(me, -2)])

    res_row = lax.dot_general(
        jnp.ones((RHS_ROWS, LANES), jnp.float32),
        acc[...],
        (((1,), (1,)), ((), ())),
        precision=HIGHEST,
        preferred_element_type=jnp.float32,
    )
    res_x[x] = jnp.concatenate(
        [res_row[0:1, i * LANES : (i + 1) * LANES] for i in range(BLOCKS)]
        + [jnp.zeros((RHS_ROWS - BLOCKS, LANES), jnp.float32)],
        axis=0,
    )
    res_copies = [push(res_x.at[x], res_x.at[x], "x", s) for s in (1, 2, 3)]

    x_copies = []
    for q in range(4):
        rows = block_at(near + 1 + q)
        arrive(fold_copies[q])
        for step, side in ((1, 0), (3, 1)):
            index = (x + step) % 4
            there = half_of(rows, side)
            part[index, there, :] = part[index, there, :] + fold_in[side, there, :]
        x_copies.append(
            [push(part.at[(x + s) % 4, rows, :], x_in.at[side, rows, :], "x", s) for s, side in ((1, 0), (3, 1))]
        )
    pl.semaphore_wait(known_sem.at[1], 2)
    vouch(2, [along_z(me, 4), along_z(me, -4)])

    near_copies = []
    for q in range(4):
        rows = block_at(near + 1 + q)
        arrive(x_copies[q])
        summed = part[x, rows, :] + x_in[0, rows, :] + x_in[1, rows, :]
        if q < 3:
            x_sum[rows, :] = summed
            near_copies.append(push(x_sum.at[rows, :], near_in.at[near], "near", q + 1))
        else:
            near_in[near] = summed
        if q == 1:
            arrive(res_copies)
            res_near[near] = res_x[0] + res_x[1] + res_x[2] + res_x[3]
            res_copies = [push(res_near.at[near], res_near.at[near], "near", s) for s in (1, 2, 3)]
    arrive(near_copies)
    near_sum[...] = near_in[0] + near_in[1] + near_in[2] + near_in[3]

    pl.semaphore_wait(known_sem.at[2], 2)
    far_copies = []
    for s in (2, 1, 3):
        rows = rows_at((far + s) % 4 * CHUNK, CHUNK, CHUNK)
        far_copies.append(push(near_sum.at[rows, :], far_in.at[far], "far", s))
    far_in[far] = near_sum[rows_at(far * CHUNK, CHUNK, CHUNK), :]
    drain(6)
    arrive(res_copies)
    res_far[far] = res_near[0] + res_near[1] + res_near[2] + res_near[3]
    res_copies = [push(res_far.at[far], res_far.at[far], "far", s) for s in (1, 2, 3)]
    arrive(far_copies)

    def chunk_of(at_near, at_far):
        rows = rows_at(at_near % 4 * BLOCK + at_far % 4 * CHUNK, CHUNK, CHUNK)
        return cols_ref.at[x, rows, :]

    own = chunk_of(near, far)
    own[...] = (far_in[0] + far_in[1] + far_in[2] + far_in[3]) * scaling

    far_copies = {s: push(own, own, "far", s) for s in (2, 1, 3)}
    near_copies = [push(own, own, "near", s) for s in (2, 1, 3)]
    arrive(res_copies)
    rhs_ref[...] = (res_far[0] + res_far[1] + res_far[2] + res_far[3]) * scaling
    for s in (1, 3, 2):
        arrive([far_copies[s]])
        chunk = chunk_of(near, far - s + 4)
        near_copies += [push(chunk, chunk, "near", t) for t in (2, 1, 3)]

    def share(step):
        block = cols_ref.at[x, block_at(near + step), :]
        cols_copies.append([push(block, block, "x", t) for t in (1, 3)])

    def share_on(step):
        arrive(cols_copies[step])
        for t, side in ((1, 0), (3, 1)):
            there = cols_ref.at[(x - t + 4) % 4, half_of(block_at(near + step), side), :]
            on_copies.append(push(there, there, "x", t))

    cols_copies = []
    on_copies = []
    share(0)
    drain(14)
    arrive(near_copies)
    share(1)

    values = cols_ref[x]
    high = values.astype(jnp.bfloat16)
    low = (values - high.astype(jnp.float32)).astype(jnp.bfloat16)
    lhs[:, 0:LANES] = high
    lhs[:, LANES : 2 * LANES] = high
    lhs[:, 2 * LANES :] = low
    rhs_t[:, 0:LANES] = high
    rhs_t[:, LANES : 2 * LANES] = low
    rhs_t[:, 2 * LANES :] = high
    for pair in range(BLOCKS // 2):
        first, width = pair * 2 * LANES, (pair + 1) * 2 * LANES
        product = lax.dot_general(
            lhs[first:width, :],
            rhs_t[0:width, :],
            (((1,), (1,)), ((), ())),
            preferred_element_type=jnp.float32,
        )
        for i in (2 * pair, 2 * pair + 1):
            for j in range(i + 1):
                base = (i * (i + 1) // 2 + j) * LANES
                tri[base : base + LANES, :] = product[
                    i * LANES - first : (i + 1) * LANES - first, j * LANES : (j + 1) * LANES
                ]
    base = BLOCKS * (BLOCKS + 1) // 2 * LANES
    tri[base:, :] = jnp.zeros((TRI_ROWS - base, LANES), jnp.float32)

    half = core * HALF
    other = (1 - core) * HALF
    spans = ((0, PART_A), (PART_A, PART_B))
    core_copies = [
        push(tri.at[rows_at(other + first, count), :], core_in.at[first : first + count, :], "core", 1)
        for first, count in spans
    ]
    orders = (("x", "y", x, y, k_in_a, l_out_a, l_in_a), ("y", "x", y, x, k_in_b, l_out_b, l_in_b))

    first_copies = []
    for (first, count), copy, (axis, _, index, _, k_in, _, _) in zip(spans, core_copies, orders):
        arrive([copy])
        k_out[first : first + count, :] = tri[rows_at(half + first, count), :] + core_in[first : first + count, :]
        strip = count // 4
        first_copies.append(
            [
                push(k_out.at[rows_at(first + (index + s) % 4 * strip, strip), :], k_in.at[index], axis, s)
                for s in (2, 1, 3)
            ]
        )
        k_in[index] = k_out[rows_at(first + index * strip, strip), :]
    share_on(0)
    share(2)
    share(3)
    second_copies = []
    for (first, count), copies, (_, axis, _, index, k_in, l_out, l_in) in zip(spans, first_copies, orders):
        strip = count // 16
        arrive(copies)
        l_out[...] = k_in[0] + k_in[1] + k_in[2] + k_in[3]
        second_copies.append(
            [push(l_out.at[rows_at((index + s) % 4 * strip, strip), :], l_in.at[index], axis, s) for s in (2, 1, 3)]
        )
        l_in[index] = l_out[rows_at(index * strip, strip), :]
    share_on(1)
    drain(12)
    second_back = []
    for (first, count), copies, (_, axis, outer, inner, _, _, l_in) in zip(spans, second_copies, orders):
        strip = count // 16
        arrive(copies)
        piece = tri_ref.at[rows_at(half + first + outer * (count // 4) + inner * strip, strip), :]
        piece[...] = l_in[0] + l_in[1] + l_in[2] + l_in[3]
        second_back.append([push(piece, piece, axis, s) for s in (2, 1, 3)])
    share_on(2)
    share_on(3)

    def quarter(first, count, index):
        return tri_ref.at[rows_at(half + first + index % 4 * (count // 4), count // 4), :]

    first_back = []
    last_copies = []
    for (first, count), copies, (axis, _, outer, _, _, _, _) in zip(spans, second_back, orders):
        arrive(copies)
        piece = quarter(first, count, outer)
        first_back.append([push(piece, piece, axis, s) for s in (2, 1, 3)])
        last_copies.append(push(piece, piece, "core", 1))
    drain(18)
    for (first, count), copies, (_, _, outer, _, _, _, _) in zip(spans, first_back, orders):
        for s, copy in zip((2, 1, 3), copies):
            arrive([copy])
            piece = quarter(first, count, outer - s + 4)
            last_copies.append(push(piece, piece, "core", 1))
    assert used[0] == COPIES
    arrive(last_copies)
    arrive(on_copies)
    drain(0)


COPIES = 96


def gather(jacobian, coded, residual, scaling):
    f32 = jnp.float32
    shapes = [
        ((DEV_ROWS, DEV_COLS), jnp.bfloat16),
        ((SKETCH, DEV_ROWS), jnp.bfloat16),
        ((SKETCH, LANES), f32),
        ((4, SKETCH, LANES), f32),
        ((2, SKETCH, LANES), f32),
        ((2, SKETCH, LANES), f32),
        ((SKETCH, LANES), f32),
        ((4, BLOCK, LANES), f32),
        ((BLOCK, LANES), f32),
        ((4, CHUNK, LANES), f32),
        ((4, RHS_ROWS, LANES), f32),
        ((4, RHS_ROWS, LANES), f32),
        ((4, RHS_ROWS, LANES), f32),
        ((SKETCH, 3 * LANES), jnp.bfloat16),
        ((SKETCH, 3 * LANES), jnp.bfloat16),
        ((TRI_ROWS, LANES), f32),
        ((HALF, LANES), f32),
        ((HALF, LANES), f32),
        ((4, PART_A // 4, LANES), f32),
        ((4, PART_B // 4, LANES), f32),
        ((PART_A // 4, LANES), f32),
        ((PART_B // 4, LANES), f32),
        ((4, PART_A // 16, LANES), f32),
        ((4, PART_B // 16, LANES), f32),
    ]
    return pl.pallas_call(
        functools.partial(gather_kernel, scaling),
        out_shape=(
            jax.ShapeDtypeStruct((TRI_ROWS, LANES), f32),
            jax.ShapeDtypeStruct((RHS_ROWS, LANES), f32),
            jax.ShapeDtypeStruct((4, SKETCH, LANES), f32),
        ),
        in_specs=[pl.BlockSpec(memory_space=pl.ANY), pl.BlockSpec(memory_space=pltpu.VMEM), pl.BlockSpec(memory_space=pltpu.VMEM)],
        out_specs=[pl.BlockSpec(memory_space=pltpu.VMEM)] * 3,
        scratch_shapes=[pltpu.VMEM(shape, kind) for shape, kind in shapes]
        + [
            pltpu.SemaphoreType.REGULAR((3,)),
            pltpu.SemaphoreType.DMA,
            pltpu.SemaphoreType.DMA((COPIES,)),
            pltpu.SemaphoreType.DMA((COPIES,)),
        ],
        compiler_params=pltpu.CompilerParams(
            collective_id=0, has_side_effects=True, vmem_limit_bytes=50 * 1024 * 1024
        ),
        name="sketch_and_kernel",
    )(jacobian, coded, residual)


def total_of(row):
    return jnp.sum(row, axis=(0, 1), keepdims=True)


def solve_kernel(tri_ref, rhs_ref, cols_ref, out_ref, rows_ref, mat, column, answer):
    me = place()
    first = pl.multiple_of(me["near"] * BLOCK + me["far"] * CHUNK, CHUNK)
    for lane in range(4):
        chunk = cols_ref[lane, pl.ds(first, CHUNK), :]
        mine = chunk[:OWN_ROWS]
        for i in range(1, 4):
            mine = jnp.where(me["x"] == i, chunk[i * OWN_ROWS : (i + 1) * OWN_ROWS], mine)
        rows_ref[:, lane * LANES : (lane + 1) * LANES] = mine

    base = 0
    eye = (
        lax.broadcasted_iota(jnp.int32, (LANES, LANES), 0) == lax.broadcasted_iota(jnp.int32, (LANES, LANES), 1)
    ).astype(jnp.float32) * 0.5
    for i in range(BLOCKS):
        for j in range(i + 1):
            block = tri_ref[base : base + LANES, :] * (1.0 / PARAMS)
            base += LANES
            if i == j:
                block = block + eye
            mat[i * LANES : (i + 1) * LANES, j * LANES : (j + 1) * LANES] = block
            if i != j:
                mat[j * LANES : (j + 1) * LANES, i * LANES : (i + 1) * LANES] = block.T

    raw = jnp.concatenate([rhs_ref[i : i + 1, :] for i in range(BLOCKS)], axis=1)
    largest = jnp.max(jnp.abs(raw), axis=(0, 1), keepdims=True)
    unit = jnp.where(largest > 0, largest, 1.0)
    rhs = raw / unit

    def to_column(row):
        for i in range(BLOCKS):
            piece = jnp.broadcast_to(row[:, i * LANES : (i + 1) * LANES], (LANES, LANES))
            column[i * LANES : (i + 1) * LANES, :] = piece.T

    def product(row):
        to_column(row)
        sums = [jnp.zeros((8, LANES), jnp.float32) for _ in range(BLOCKS)]
        for group in range(SKETCH // 8):
            rows = slice(group * 8, group * 8 + 8)
            weight = column[rows, :]
            for i in range(BLOCKS):
                sums[i] = sums[i] + weight * mat[rows, i * LANES : (i + 1) * LANES]
        return jnp.concatenate([jnp.sum(s, axis=0, keepdims=True) for s in sums], axis=1)

    def met(sol, res, tol):
        scale = total_of(sol * (rhs - res)) - 0.5 * total_of(sol * sol)
        return (tol * tol * scale - 2.0 * total_of(res * res))[0, 0] >= 0.0

    def step(_, carry):
        sol, res, way = carry
        image = product(way)
        size = total_of(res * res)
        curve = total_of(way * image)
        cross = total_of(res * image)
        square = total_of(image * image)
        alpha = jnp.where(curve > 0, size / curve, 0.0)
        new_size = jnp.maximum(size + alpha * (alpha * square - 2.0 * cross), 0.0)
        beta = jnp.where(size > 0, new_size / size, 0.0)
        res = res - alpha * image
        return (sol + alpha * way, res, res + beta * way)

    def round_of(carry):
        count, _, state = carry
        state = lax.fori_loop(0, jnp.where(count == 0, FIRST_STEPS, ROUND_STEPS), step, state)
        return (count + 1, met(state[0], state[1], STOP_TOL), state)

    def go_on(carry):
        count, done, _ = carry
        return jnp.logical_and(count < MAX_ROUNDS, jnp.logical_not(done))

    start = (jnp.zeros_like(rhs), rhs, rhs)
    first_done = largest[0, 0] <= 0.0
    _, _, (sol, _, _) = lax.while_loop(go_on, round_of, (0, first_done, start))
    true_res = rhs - product(sol)
    good = met(sol, true_res, ACCEPT_TOL)
    answer[...] = column[...]

    @pl.when(jnp.logical_not(good))
    def _():
        to_column(rhs)
        answer[...] = column[...]
        lanes = lax.broadcasted_iota(jnp.int32, (8, SKETCH), 1)
        below = lax.broadcasted_iota(jnp.int32, (8, LANES), 0)

        def pivot(k, carry):
            pivot_row = mat[pl.ds(k, 1), :]
            pivot_rhs = answer[pl.ds(k, 1), :]
            inverse = 1.0 / jnp.sum(jnp.where(lanes[0:1] == k, pivot_row, 0.0), axis=1, keepdims=True)

            def rows_of(group, inner):
                first = pl.multiple_of(group * 8, 8)
                here = mat[pl.ds(first, 8), :]
                factor = jnp.sum(jnp.where(lanes == k, here, 0.0), axis=1, keepdims=True) * inverse
                factor = jnp.where(below[:, 0:1] + first == k, 0.0, factor)
                mat[pl.ds(first, 8), :] = here - factor * pivot_row
                answer[pl.ds(first, 8), :] = answer[pl.ds(first, 8), :] - factor * pivot_rhs
                return inner

            return lax.fori_loop(0, SKETCH // 8, rows_of, carry)

        lax.fori_loop(0, SKETCH, pivot, 0)

        def divide(group, carry):
            first = pl.multiple_of(group * 8, 8)
            here = mat[pl.ds(first, 8), :]
            row = lax.broadcasted_iota(jnp.int32, (8, SKETCH), 0) + first
            diagonal = jnp.sum(jnp.where(lanes == row, here, 0.0), axis=1, keepdims=True)
            answer[pl.ds(first, 8), :] = answer[pl.ds(first, 8), :] / diagonal
            return carry

        lax.fori_loop(0, SKETCH // 8, divide, 0)

    for lane in range(4):
        values = jnp.sum(answer[...] * cols_ref[lane], axis=0, keepdims=True)
        out_ref[:, lane * LANES : (lane + 1) * LANES] = values * (unit * (1.0 / math.sqrt(PARAMS)))


def solve(tri, rhs, cols):
    return pl.pallas_call(
        solve_kernel,
        out_shape=(
            jax.ShapeDtypeStruct((1, DEV_COLS), jnp.float32),
            jax.ShapeDtypeStruct((OWN_ROWS, DEV_COLS), jnp.float32),
        ),
        in_specs=[pl.BlockSpec(memory_space=pltpu.VMEM)] * 3,
        out_specs=[pl.BlockSpec(memory_space=pltpu.VMEM)] * 2,
        scratch_shapes=[
            pltpu.VMEM((SKETCH, SKETCH), jnp.float32),
            pltpu.VMEM((SKETCH, LANES), jnp.float32),
            pltpu.VMEM((SKETCH, LANES), jnp.float32),
        ],
        compiler_params=pltpu.CompilerParams(vmem_limit_bytes=16 * 1024 * 1024),
        name="solve",
    )(tri, rhs, cols)


def on_device(jacobian, residual, bucket, sign_bit):
    scaling = math.sqrt(SKETCH / (DEV_ROWS * 64))
    tile = (GROUPS, LANES)
    signs = (2 * sign_bit - 1).astype(jnp.float32)
    coded = (bucket.astype(jnp.float32) + 1.0) * signs
    tri, rhs, cols = gather(jacobian, coded.reshape(tile), (residual * signs).reshape(tile), scaling)
    update, rows = solve(tri, rhs, cols)
    return (update.reshape(DEV_COLS), rows)


def solution(mesh):
    return jax.shard_map(
        on_device,
        mesh=mesh,
        in_specs=(P("dp", "col"), P("dp"), P("dp"), P("dp")),
        out_specs=(P("col"), P("dp", "col")),
        check_vma=False,
    )
```
